256 devices in a mesh: row: 8 (over y, x_hi), col: 32 (over z, x_lo, core).
Axes of the slice: x: 4 (x_hi: 2, x_lo: 2; x = x_hi * 2 + x_lo), y: 4, z: 8, core: 2. Of those that a mesh axis runs over, the one named last changes fastest.
Arguments:
- reconstructor: bfloat16 [8192, 40960], P('row', 'col'), may hold values from -0.03125 to 0.03125
- slopes: bfloat16 [40960, 2048], P('col', 'row'), may hold values from -6 to 6
- commands: float32 [2048, 8192], P('col', 'row'), may hold values from -6 to 6
Outputs:
- gradient: float32 [8192, 40960], P('row', 'col')
- residual: float32 [2048, 8192], P('col', 'row')
The draws below stay inside these ranges and needn't reach their ends.
All inputs are finite; a program needn't handle non-finite values.
Results may differ from the reference program's by a relative error of at most 0.0028.
Values may be sent and summed in bfloat16 or wider, within the bound.
A program may use at most 128 MiB of HBM per device.

```python
import jax
import jax.numpy as jnp
from jax import lax

CMD = 8192
SLO = 40960
FRAMES = 2048


def shard_levels(rng, shape, split, least, top_value):
    def one(axis_at, blocks):
        steps = jax.random.uniform(jax.random.fold_in(jax.random.fold_in(rng, 6), axis_at), (blocks,), jnp.float32, least / len(split), top_value / len(split))
        return jnp.repeat(jnp.exp(steps), shape[axis_at] // blocks).reshape((-1,) + (1,) * (len(shape) - axis_at - 1))

    factor_of = one(*split[0])
    for cut in split[1:]:
        factor_of = factor_of * one(*cut)
    return factor_of


def noise(own_key, dims, deviation, most, cuts=(), held_as=jnp.bfloat16):
    values = deviation * jax.random.normal(own_key, dims, jnp.float32)
    if cuts:
        values = values * shard_levels(own_key, dims, cuts, -0.22, 0.18)
    return jnp.clip(values, -most, most).astype(held_as)


def setup_inputs(seed: int = 0) -> dict:
    splits = jax.random.split(jax.random.key(seed), 4)
    return {
        "reconstructor": noise(splits[0], (CMD, SLO), SLO ** -0.5, 0.03125, ((0, 8), (1, 32))),
        "slopes": noise(splits[1], (SLO, FRAMES), 1.0, 6.0, ((0, 32), (1, 8))),
        "commands": noise(splits[2], (FRAMES, CMD), 1.0, 6.0, ((0, 32), (1, 8)), jnp.float32),
    }


def reference(reconstructor, slopes, commands):
    predicted = lax.dot_general(slopes, reconstructor, (((0,), (1,)), ((), ())), preferred_element_type=jnp.float32)
    residual = predicted - commands
    residual_low = residual.astype(jnp.bfloat16)
    summed_frames = lax.dot_general(residual_low, slopes, (((0,), (1,)), ((), ())), preferred_element_type=jnp.float32)
    scale_factor = 1.0 / jnp.sqrt(jnp.float32(FRAMES))
    return (summed_frames * scale_factor, residual)
```

```python
import functools

import jax
import jax.numpy as jnp
from jax import lax
from jax.experimental import pallas as pl
from jax.experimental.pallas import tpu as pltpu
from jax.sharding import PartitionSpec as P

MESH = pl.DeviceIdType.MESH

FULL = 1024
HALF = 512
SLICE = 64
DEPTH = 1280
BLOCK = 256
BLOCKS = 8
STAGES = 12
LEAD = 4


def code(v):
    return (v * jnp.abs(v) * (v * v)).astype(jnp.bfloat16)


def decode(b):
    b = b.astype(jnp.float32)
    m = jnp.maximum(jnp.abs(b), 1e-36)
    m = m * lax.rsqrt(m)
    m = m * lax.rsqrt(m)
    return jnp.where(b < 0, -m, m)


def kernel(
    r_hbm, s_hbm, c_hbm, g_ref, res_ref,
    r_ref, sall, cpad, cmd_t, acc, csend, crecv, zsend, zrecv, xsend, xrecv, rall, turned,
    in_sem, s_ss, s_rs, ss, rs,
):
    row, col = lax.axis_index("row"), lax.axis_index("col")
    y, xh = row // 2, row % 2
    z, xl, core = col // 4, (col // 2) % 2, col % 2
    quad = xl * 2 + core
    y_up = (((y + 1) % 4) * 2 + xh, col)
    y_dn = (((y + 3) % 4) * 2 + xh, col)
    x_far = (y * 2 + 1 - xh, col)
    z_up = (row, ((z + 1) % 8) * 4 + quad)
    z_dn = (row, ((z + 7) % 8) * 4 + quad)
    x_near = (row, z * 4 + (1 - xl) * 2 + core)
    twin = (row, z * 4 + xl * 2 + 1 - core)

    barrier = pltpu.get_barrier_semaphore()
    for device in (y_up, y_dn, x_far, z_up, z_dn, x_near, twin):
        pl.semaphore_signal(barrier, inc=1, device_id=device, device_id_type=MESH)

    s_in = pltpu.make_async_copy(s_hbm, sall.at[0], in_sem.at[0])
    r_in = pltpu.make_async_copy(r_hbm, r_ref, in_sem.at[1])
    s_in.start()
    r_in.start()
    cpad[...] = jnp.zeros_like(cpad)
    c_in = pltpu.make_async_copy(
        c_hbm, cpad.at[pl.ds(pl.multiple_of(quad * 64, 64), 64)], in_sem.at[2]
    )
    c_in.start()

    def remote(src, dst, send, recv, device):
        return pltpu.make_async_remote_copy(
            src_ref=src, dst_ref=dst, send_sem=send, recv_sem=recv,
            device_id=device, device_id_type=MESH,
        )

    mid = DEPTH // 2
    lo, hi = pl.ds(0, mid), pl.ds(mid, mid)
    s_moves = [
        remote(sall.at[0], sall.at[1], s_ss.at[0], s_rs.at[0], y_up),
        remote(sall.at[0], sall.at[2], s_ss.at[1], s_rs.at[1], y_dn),
        remote(sall.at[0], sall.at[3], s_ss.at[2], s_rs.at[2], x_far),
        remote(sall.at[1, lo], sall.at[4, lo], s_ss.at[3], s_rs.at[3], y_up),
        remote(sall.at[2, hi], sall.at[4, hi], s_ss.at[4], s_rs.at[4], y_dn),
        remote(sall.at[3], sall.at[5], s_ss.at[5], s_rs.at[5], y_up),
        remote(sall.at[3], sall.at[6], s_ss.at[6], s_rs.at[6], y_dn),
        remote(sall.at[4], sall.at[7], s_ss.at[7], s_rs.at[7], x_far),
    ]
    s_in.wait()
    pl.semaphore_wait(barrier, 7)
    for i in (0, 1, 2):
        s_moves[i].start()

    c_in.wait()
    cmd_t[...] = cpad[...].T
    g_ref[...] = jnp.zeros_like(g_ref)
    r_in.wait()

    dy = (z // 2 + 4 - y) % 4
    dx = (z % 2 + 2 - xh) % 2
    near = jnp.where(dy == 0, 0, jnp.where(dy == 3, 1, jnp.where(dy == 1, 2, 4)))
    far = jnp.where(dy == 0, 3, jnp.where(dy == 3, 5, jnp.where(dy == 1, 6, 7)))
    my_slot = jnp.where(dx == 0, near, far)

    own0 = core * HALF
    other0 = (1 - core) * HALF

    def rows(start, size):
        return pl.ds(pl.multiple_of(start, size), size)

    def part(at):
        return rows(((z + at + 8) % 8) * SLICE, SLICE)

    def full_part(at):
        return rows(own0 + ((z + at + 8) % 8) * SLICE, SLICE)

    def core_move(g):
        return remote(csend.at[g], crecv.at[g], ss.at[g, 0], rs.at[g, 0], twin)

    def up_move(g, i):
        return remote(zsend.at[g, i], zrecv.at[g, i], ss.at[g, 1 + i], rs.at[g, 1 + i], z_up)

    def dn_move(g, i):
        return remote(
            zsend.at[g, 4 + i], zrecv.at[g, 4 + i], ss.at[g, 5 + i], rs.at[g, 5 + i], z_dn
        )

    def x_move(g):
        return remote(xsend.at[g], xrecv.at[g], ss.at[g, 8], rs.at[g, 8], x_near)

    def out_up(g, i):
        here = rall.at[g, full_part(-i)]
        return remote(here, here, ss.at[g, 9 + i], rs.at[g, 9 + i], z_up)

    def in_up(g, i):
        here = rall.at[g, full_part(-i - 1)]
        return remote(here, here, ss.at[g, 9 + i], rs.at[g, 9 + i], z_up)

    def out_dn(g, i):
        here = rall.at[g, full_part(i)]
        return remote(here, here, ss.at[g, 12 + i], rs.at[g, 12 + i], z_dn)

    def in_dn(g, i):
        here = rall.at[g, full_part(i + 1)]
        return remote(here, here, ss.at[g, 12 + i], rs.at[g, 12 + i], z_dn)

    def out_core(g):
        here = rall.at[g, rows(own0, HALF)]
        return remote(here, here, ss.at[g, 16], rs.at[g, 16], twin)

    def in_core(g):
        here = rall.at[g, rows(other0, HALF)]
        return remote(here, here, ss.at[g, 16], rs.at[g, 16], twin)

    def both(g, at):
        return acc[g, part(at), :] + decode(crecv[g, part(at), :])

    def stage_predict(g):
        @pl.when(g == 1)
        def _():
            s_moves[0].wait_recv()
            s_moves[3].start()
            s_moves[1].wait_recv()
            s_moves[4].start()
            s_moves[2].wait_recv()
            s_moves[5].start()
            s_moves[6].start()

        @pl.when(g == 4)
        def _():
            s_moves[3].wait_recv()
            s_moves[4].wait_recv()
            s_moves[7].start()

        for slot in (5, 6, 7):

            @pl.when(g == slot)
            def _(slot=slot):
                s_moves[slot].wait_recv()

        mine = (g == my_slot).astype(jnp.float32)
        tile = 256

        def predicted(start):
            p = jnp.dot(
                r_ref[rows(start, tile), :], sall[g], preferred_element_type=jnp.float32
            )
            return p - cmd_t[rows(start, tile), :] * mine

        @pl.loop(0, HALF // tile)
        def _(i):
            csend[g, rows(i * tile, tile), :] = code(predicted(other0 + i * tile))

        core_move(g).start()

        @pl.loop(0, HALF // tile)
        def _(i):
            acc[g, rows(i * tile, tile), :] = predicted(own0 + i * tile)

    def stage_1(g):
        core_move(g).wait_recv()
        zsend[g, 0] = code(both(g, 4))
        up_move(g, 0).start()

    def stage_2(g):
        zsend[g, 4] = code(both(g, -3))
        dn_move(g, 0).start()
        up_move(g, 0).wait_recv()
        zsend[g, 1] = code(both(g, 3) + decode(zrecv[g, 0]))
        up_move(g, 1).start()

    def stage_3(g):
        dn_move(g, 0).wait_recv()
        zsend[g, 5] = code(both(g, -2) + decode(zrecv[g, 4]))
        dn_move(g, 1).start()
        up_move(g, 1).wait_recv()
        zsend[g, 2] = code(both(g, 2) + decode(zrecv[g, 1]))
        up_move(g, 2).start()

    def stage_4(g):
        dn_move(g, 1).wait_recv()
        zsend[g, 6] = code(both(g, -1) + decode(zrecv[g, 5]))
        dn_move(g, 2).start()
        up_move(g, 2).wait_recv()
        zsend[g, 3] = code(both(g, 1) + decode(zrecv[g, 2]))
        up_move(g, 3).start()

    def stage_5(g):
        dn_move(g, 2).wait_recv()
        up_move(g, 3).wait_recv()
        total = both(g, 0) + decode(zrecv[g, 6]) + decode(zrecv[g, 3])
        acc[g, part(0), :] = total
        xsend[g] = code(total)
        x_move(g).start()

    def stage_6(g):
        x_move(g).wait_recv()
        low = (acc[g, part(0), :] + decode(xrecv[g])).astype(jnp.bfloat16)
        rall[g, full_part(0), :] = low
        out_dn(g, 0).start()
        out_up(g, 0).start()

    def stage_7(g):
        in_dn(g, 0).wait_recv()
        out_dn(g, 1).start()
        in_up(g, 0).wait_recv()
        out_up(g, 1).start()

    def stage_8(g):
        in_dn(g, 1).wait_recv()
        out_dn(g, 2).start()
        in_up(g, 1).wait_recv()
        out_up(g, 2).start()

    def stage_9(g):
        in_dn(g, 2).wait_recv()
        out_dn(g, 3).start()
        in_up(g, 2).wait_recv()

    def stage_10(g):
        in_dn(g, 3).wait_recv()
        out_core(g).start()

    def stage_gradient(g):
        in_core(g).wait_recv()
        tile = 256

        @pl.loop(0, FULL // tile)
        def _(i):
            g_ref[rows(i * tile, tile), :] += lax.dot_general(
                rall[g, rows(i * tile, tile), :], sall[g],
                (((1,), (1,)), ((), ())), preferred_element_type=jnp.float32,
            )

        @pl.when(g == my_slot)
        def _():
            half = rall[g, :, pl.ds(pl.multiple_of(xl * 128, 128), 128)]
            turned[...] = half.astype(jnp.float32).T
            res_ref[...] = turned[rows(core * 64, 64), :]

        core_move(g).wait_send()
        for i in range(4):
            up_move(g, i).wait_send()
            out_dn(g, i).wait_send()
        for i in range(3):
            dn_move(g, i).wait_send()
            out_up(g, i).wait_send()
        x_move(g).wait_send()
        out_core(g).wait_send()

    stages = [
        stage_predict, stage_1, stage_2, stage_3, stage_4, stage_5, stage_6,
        stage_7, stage_8, stage_9, stage_10, stage_gradient,
    ]
    order = [10, 9, 8, 7, 6, 5, 4, 3, 2, 1, 0, 11]

    def tick(t, carry):
        for k in order:
            u = t - k
            g = jnp.where(u <= 0, 0, u - LEAD)
            active = (u == 0) | ((u > LEAD) & (u < BLOCKS + LEAD))

            @pl.when(active)
            def _(k=k, g=g):
                stages[k](g)

        return carry

    lax.fori_loop(0, BLOCKS + LEAD + STAGES - 1, tick, 0)
    for move in s_moves:
        move.wait_send()


def on_device(reconstructor, slopes, commands):
    vmem = pltpu.VMEM
    gradient, residual = pl.pallas_call(
        kernel,
        out_shape=(
            jax.ShapeDtypeStruct((FULL, DEPTH), jnp.float32),
            jax.ShapeDtypeStruct((64, FULL), jnp.float32),
        ),
        in_specs=[pl.BlockSpec(memory_space=pl.ANY)] * 3,
        out_specs=[pl.BlockSpec(memory_space=pltpu.VMEM)] * 2,
        scratch_shapes=[
            vmem((FULL, DEPTH), jnp.bfloat16),
            vmem((BLOCKS, DEPTH, BLOCK), jnp.bfloat16),
            vmem((BLOCK, FULL), jnp.float32),
            vmem((FULL, BLOCK), jnp.float32),
            vmem((BLOCKS, HALF, BLOCK), jnp.float32),
            vmem((BLOCKS, HALF, BLOCK), jnp.bfloat16),
            vmem((BLOCKS, HALF, BLOCK), jnp.bfloat16),
            vmem((BLOCKS, 7, SLICE, BLOCK), jnp.bfloat16),
            vmem((BLOCKS, 7, SLICE, BLOCK), jnp.bfloat16),
            vmem((BLOCKS, SLICE, BLOCK), jnp.bfloat16),
            vmem((BLOCKS, SLICE, BLOCK), jnp.bfloat16),
            vmem((BLOCKS, FULL, BLOCK), jnp.bfloat16),
            vmem((128, FULL), jnp.float32),
            pltpu.SemaphoreType.DMA((3,)),
            pltpu.SemaphoreType.DMA((8,)),
            pltpu.SemaphoreType.DMA((8,)),
            pltpu.SemaphoreType.DMA((BLOCKS, 17)),
            pltpu.SemaphoreType.DMA((BLOCKS, 17)),
        ],
        compiler_params=pltpu.CompilerParams(
            collective_id=0, has_side_effects=True, vmem_limit_bytes=56 << 20
        ),
        cost_estimate=pl.CostEstimate(
            flops=4 * 2048 * FULL * DEPTH, bytes_accessed=9 << 20, transcendentals=0
        ),
    )(reconstructor, slopes, commands)
    scale_factor = 1.0 / jnp.sqrt(jnp.float32(2048))
    return gradient * scale_factor, residual


def solution(mesh):
    in_specs = (P("row", "col"), P("col", "row"), P("col", "row"))
    out_specs = (P("row", "col"), P("col", "row"))
    return jax.shard_map(
        on_device, mesh=mesh, in_specs=in_specs, out_specs=out_specs, check_vma=False
    )
```

```python
import functools

import jax
import jax.numpy as jnp
from jax import lax
from jax.experimental import pallas as pl
from jax.experimental.pallas import tpu as pltpu
from jax.sharding import PartitionSpec as P

MESH = pl.DeviceIdType.MESH

FULL = 1024
HALF = 512
SLICE = 64
DEPTH = 1280
BLOCK = 256
BLOCKS = 8
WHEN = (
    (0, 3, 6, 10, 15, 18, 21, 24),
    (1, 4, 8, 11, 16, 20, 22, 25),
    (2, 7, 17, 18, 19, 23, 26, 30),
    (5, 12, 19, 21, 29, 28, 32, 34),
    (8, 18, 23, 24, 31, 32, 33, 35),
    (13, 20, 29, 30, 35, 36, 37, 39),
    (20, 27, 38, 34, 39, 40, 41, 42),
    (20, 27, 38, 36, 39, 41, 42, 43),
)
SEND_ON = (3, 6, 9, 10, 14, 15)


def code(v):
    return (v * jnp.abs(v) * (v * v)).astype(jnp.bfloat16)


def decode(b):
    b = b.astype(jnp.float32)
    m = jnp.maximum(jnp.abs(b), 1e-36)
    m = m * lax.rsqrt(m)
    m = m * lax.rsqrt(m)
    return jnp.where(b < 0, -m, m)


def kernel(
    r_hbm, s_hbm, c_hbm, g_ref, res_ref,
    r_ref, sall, cpad, cmd_t, acc, csend, crecv, near_s, near_r, far_s, far_r, sum_s, sum_r,
    xsend, xrecv, rall, turned,
    in_sem, s_ss, s_rs, ss, rs,
):
    row, col = lax.axis_index("row"), lax.axis_index("col")
    y, xh = row // 2, row % 2
    z, xl, core = col // 4, (col // 2) % 2, col % 2
    quad = xl * 2 + core
    y_up = (((y + 1) % 4) * 2 + xh, col)
    y_dn = (((y + 3) % 4) * 2 + xh, col)
    x_far = (y * 2 + 1 - xh, col)
    z_up = (row, ((z + 1) % 8) * 4 + quad)
    z_dn = (row, ((z + 7) % 8) * 4 + quad)
    z_up2 = (row, ((z + 2) % 8) * 4 + quad)
    z_dn2 = (row, ((z + 6) % 8) * 4 + quad)
    x_near = (row, z * 4 + (1 - xl) * 2 + core)
    twin = (row, z * 4 + xl * 2 + 1 - core)

    barrier = pltpu.get_barrier_semaphore()
    for device in (y_up, y_dn, x_far, z_up, z_dn, z_up2, z_dn2, x_near, twin):
        pl.semaphore_signal(barrier, inc=1, device_id=device, device_id_type=MESH)

    s_in = pltpu.make_async_copy(s_hbm, sall.at[0], in_sem.at[0])
    r_in = pltpu.make_async_copy(r_hbm, r_ref, in_sem.at[1])
    s_in.start()
    r_in.start()
    cpad[...] = jnp.zeros_like(cpad)
    def remote(src, dst, send, recv, device):
        return pltpu.make_async_remote_copy(
            src_ref=src, dst_ref=dst, send_sem=send, recv_sem=recv,
            device_id=device, device_id_type=MESH,
        )

    mid = DEPTH // 2
    lo, hi, every = pl.ds(0, mid), pl.ds(mid, mid), pl.ds(0, DEPTH)
    left, right = pl.ds(0, 128), pl.ds(128, 128)
    s_moves = [
        remote(sall.at[i, r0, c0], sall.at[j, r0, c1], s_ss.at[n], s_rs.at[n], device)
        for n, (i, j, r0, c0, c1, device) in enumerate((
            (0, 1, every, left, left, y_up),
            (0, 1, every, left, right, y_dn),
            (0, 2, every, right, left, y_up),
            (0, 2, every, right, right, y_dn),
            (0, 3, every, left, left, x_far),
            (0, 3, every, right, right, x_far),
            (1, 4, lo, left, left, y_up),
            (1, 4, hi, right, left, y_dn),
            (2, 4, lo, left, right, y_up),
            (2, 4, hi, right, right, y_dn),
            (3, 5, every, left, left, y_up),
            (3, 5, every, left, right, y_dn),
            (3, 6, every, right, left, y_up),
            (3, 6, every, right, right, y_dn),
            (4, 7, every, left, left, x_far),
            (4, 7, every, right, right, x_far),
        ))
    ]
    passes = [
        ((0, 1), (6, 7)), ((2, 3), (8, 9)), ((4,), (10, 11)), ((5,), (12, 13)), ((6, 7), (14,)),
        ((8, 9), (15,)),
    ]
    dy = (z // 2 + 4 - y) % 4
    dx = (z % 2 + 2 - xh) % 2
    beside = (dy == 1) | (dy == 3)
    my_slot = jnp.where(beside, 1 + 4 * dx + xl, jnp.where(dy == 0, 3 * dx, 4 + 3 * dx))
    my_half = jnp.where(beside, (dy == 1).astype(jnp.int32), xl)
    c_in = pltpu.make_async_copy(
        c_hbm,
        cpad.at[pl.ds(pl.multiple_of(my_half * 128 + core * 64, 64), 64)],
        in_sem.at[2],
    )
    c_in.start()
    s_in.wait()
    pl.semaphore_wait(barrier, 9)
    for i in (0, 1, 4, 2, 3, 5):
        s_moves[i].start()

    c_in.wait()
    cmd_t[...] = cpad[...].T
    g_ref[...] = jnp.zeros_like(g_ref)
    r_in.wait()

    own0 = core * HALF
    other0 = (1 - core) * HALF

    def rows(start, size):
        return pl.ds(pl.multiple_of(start, size), size)

    def part(at, size=SLICE, skip=0):
        return rows(((z + at + 8) % 8) * SLICE + skip, size)

    def full_part(at, size=SLICE, skip=0):
        return rows(own0 + ((z + at + 8) % 8) * SLICE + skip, size)

    def core_move(g):
        return remote(csend.at[g], crecv.at[g], ss.at[g, 0], rs.at[g, 0], twin)

    one, two = (z_up, z_dn), (z_up2, z_dn2)

    def near_move(g, d):
        return remote(near_s.at[g, d], near_r.at[g, d], ss.at[g, 1 + d], rs.at[g, 1 + d], one[d])

    def far_move(g, d):
        return remote(far_s.at[g, d], far_r.at[g, d], ss.at[g, 3 + d], rs.at[g, 3 + d], two[d])

    def sum_move(g, d):
        return remote(sum_s.at[g, d], sum_r.at[g, d], ss.at[g, 5 + d], rs.at[g, 5 + d], two[d])

    def x_move(g):
        return remote(xsend.at[g], xrecv.at[g], ss.at[g, 7], rs.at[g, 7], x_near)

    def spread(g, d, n, at, device, size=SLICE, skip=0):
        here = rall.at[g, full_part(at, size, skip)]
        return remote(here, here, ss.at[g, n + d], rs.at[g, n + d], device)

    def out_1(g, d):
        return spread(g, d, 8, 0, one[d])

    def in_1(g, d):
        return spread(g, d, 8, (-1, 1)[d], one[d])

    def out_2(g, d):
        return spread(g, d, 10, 0, two[d])

    def in_2(g, d):
        return spread(g, d, 10, (-2, 2)[d], two[d])

    def out_3(g, d):
        return spread(g, d, 12, (-2, 2)[d], one[d])

    def in_3(g, d):
        return spread(g, d, 12, (-3, 3)[d], one[d])

    def out_4(g, d):
        return spread(g, d, 14, (-2, 2)[d], two[d], SLICE // 2, d * SLICE // 2)

    def in_4(g, d):
        return spread(g, d, 14, 4, two[d], SLICE // 2, d * SLICE // 2)

    def out_core(g):
        here = rall.at[g, rows(own0, HALF)]
        return remote(here, here, ss.at[g, 16], rs.at[g, 16], twin)

    def in_core(g):
        here = rall.at[g, rows(other0, HALF)]
        return remote(here, here, ss.at[g, 16], rs.at[g, 16], twin)

    def both(g, at, size=SLICE, skip=0):
        here = part(at, size, skip)
        return acc[g, here, :] + decode(crecv[g, here, :])

    def pass_on(n):
        arrived, onward = passes[n]
        for i in arrived:
            s_moves[i].wait_recv()
        for i in onward:
            s_moves[i].start()

    def stage_predict(g):
        for slot in (5, 6, 7):

            @pl.when(g == slot)
            def _(slot=slot):
                s_moves[2 * slot].wait_recv()
                s_moves[2 * slot + 1].wait_recv()

        mine = (g == my_slot).astype(jnp.float32)
        tile = 512

        def predicted(start):
            p = jnp.dot(
                r_ref[rows(start, tile), :], sall[g], preferred_element_type=jnp.float32
            )
            return p - cmd_t[rows(start, tile), :] * mine

        @pl.loop(0, HALF // tile)
        def _(i):
            csend[g, rows(i * tile, tile), :] = code(predicted(other0 + i * tile))

        core_move(g).start()

        @pl.loop(0, HALF // tile)
        def _(i):
            acc[g, rows(i * tile, tile), :] = predicted(own0 + i * tile)

    half = SLICE // 2
    first, second = pl.ds(0, SLICE), pl.ds(SLICE, SLICE)

    def stage_1(g):
        core_move(g).wait_recv()
        for d, sign in ((0, 1), (1, -1)):
            far_s[g, d] = code(both(g, 4, half, d * half))
            far_move(g, d).start()
            near_s[g, d, second, :] = code(both(g, 3 * sign))
            near_s[g, d, first, :] = code(both(g, sign))
            near_move(g, d).start()

    def stage_2(g):
        for d, sign in ((0, 1), (1, -1)):
            near_move(g, d).wait_recv()
            far_move(g, d).wait_recv()
            for h in (0, 1):
                total = both(g, 2 * sign, half, h * half) + decode(
                    near_r[g, d, pl.ds(SLICE + h * half, half), :]
                )
                if h == d:
                    total = total + decode(far_r[g, d])
                sum_s[g, d, pl.ds(h * half, half), :] = code(total)
            sum_move(g, d).start()

    def stage_3(g):
        total = both(g, 0) + decode(near_r[g, 0, first, :]) + decode(near_r[g, 1, first, :])
        for d in (0, 1):
            sum_move(g, d).wait_recv()
            total = total + decode(sum_r[g, d])
        acc[g, part(0), :] = total
        xsend[g] = code(total)
        x_move(g).start()

    def stage_4(g):
        x_move(g).wait_recv()
        low = (acc[g, part(0), :] + decode(xrecv[g])).astype(jnp.bfloat16)
        rall[g, full_part(0), :] = low
        for d in (0, 1):
            out_2(g, d).start()
        for d in (0, 1):
            out_1(g, d).start()

    def stage_5(g):
        for d in (0, 1):
            in_2(g, d).wait_recv()
            out_4(g, d).start()
            out_3(g, d).start()

    def add_gradient(g, start):
        here = rows(start, HALF)
        g_ref[here, :] += lax.dot_general(
            rall[g, here, :], sall[g], (((1,), (1,)), ((), ())),
            preferred_element_type=jnp.float32,
        )

    def stage_6(g):
        for d in (0, 1):
            in_1(g, d).wait_recv()
            in_3(g, d).wait_recv()
            in_4(g, d).wait_recv()
        out_core(g).start()
        add_gradient(g, own0)

    def stage_gradient(g):
        in_core(g).wait_recv()
        add_gradient(g, other0)

        @pl.when(g == my_slot)
        def _():
            half = rall[g, :, pl.ds(pl.multiple_of(my_half * 128, 128), 128)]
            turned[...] = half.astype(jnp.float32).T
            res_ref[...] = turned[rows(core * 64, 64), :]

        core_move(g).wait_send()
        for move in (near_move, far_move, sum_move, out_1, out_2, out_3, out_4):
            for d in (0, 1):
                move(g, d).wait_send()
        x_move(g).wait_send()
        out_core(g).wait_send()

    stages = [
        stage_predict, stage_1, stage_2, stage_3, stage_4, stage_5, stage_6, stage_gradient,
    ]
    order = [6, 5, 4, 3, 2, 1, 0, 7]

    def tick(t, carry):
        for n, at in enumerate(SEND_ON):
            pl.when(t == at)(functools.partial(pass_on, n))
        for k in order:
            g, active = jnp.int32(0), t == WHEN[k][0]
            for i in range(1, BLOCKS):
                g = jnp.where(t == WHEN[k][i], i, g)
                active = active | (t == WHEN[k][i])

            @pl.when(active)
            def _(k=k, g=g):
                stages[k](g)

        return carry

    lax.fori_loop(0, max(WHEN[-1]) + 1, tick, 0)
    for move in s_moves:
        move.wait_send()


def on_device(reconstructor, slopes, commands):
    vmem = pltpu.VMEM
    gradient, residual = pl.pallas_call(
        kernel,
        out_shape=(
            pltpu.VMEM((FULL, DEPTH), jnp.float32),
            pltpu.VMEM((64, FULL), jnp.float32),
        ),
        in_specs=[pl.BlockSpec(memory_space=pl.ANY)] * 3,
        out_specs=[pl.BlockSpec(memory_space=pltpu.VMEM)] * 2,
        scratch_shapes=[
            vmem((FULL, DEPTH), jnp.bfloat16),
            vmem((BLOCKS, DEPTH, BLOCK), jnp.bfloat16),
            vmem((BLOCK, FULL), jnp.float32),
            vmem((FULL, BLOCK), jnp.float32),
            vmem((BLOCKS, HALF, BLOCK), jnp.float32),
            vmem((BLOCKS, HALF, BLOCK), jnp.bfloat16),
            vmem((BLOCKS, HALF, BLOCK), jnp.bfloat16),
            vmem((BLOCKS, 2, 2 * SLICE, BLOCK), jnp.bfloat16),
            vmem((BLOCKS, 2, 2 * SLICE, BLOCK), jnp.bfloat16),
            vmem((BLOCKS, 2, SLICE // 2, BLOCK), jnp.bfloat16),
            vmem((BLOCKS, 2, SLICE // 2, BLOCK), jnp.bfloat16),
            vmem((BLOCKS, 2, SLICE, BLOCK), jnp.bfloat16),
            vmem((BLOCKS, 2, SLICE, BLOCK), jnp.bfloat16),
            vmem((BLOCKS, SLICE, BLOCK), jnp.bfloat16),
            vmem((BLOCKS, SLICE, BLOCK), jnp.bfloat16),
            vmem((BLOCKS, FULL, BLOCK), jnp.bfloat16),
            vmem((128, FULL), jnp.float32),
            pltpu.SemaphoreType.DMA((3,)),
            pltpu.SemaphoreType.DMA((16,)),
            pltpu.SemaphoreType.DMA((16,)),
            pltpu.SemaphoreType.DMA((BLOCKS, 17)),
            pltpu.SemaphoreType.DMA((BLOCKS, 17)),
        ],
        compiler_params=pltpu.CompilerParams(
            collective_id=0, has_side_effects=True, vmem_limit_bytes=56 << 20
        ),
        cost_estimate=pl.CostEstimate(
            flops=4 * 2048 * FULL * DEPTH, bytes_accessed=9 << 20, transcendentals=0
        ),
    )(reconstructor, slopes, commands)
    scale_factor = 1.0 / jnp.sqrt(jnp.float32(2048))
    return gradient * scale_factor, residual


def solution(mesh):
    in_specs = (P("row", "col"), P("col", "row"), P("col", "row"))
    out_specs = (P("row", "col"), P("col", "row"))
    return jax.shard_map(
        on_device, mesh=mesh, in_specs=in_specs, out_specs=out_specs, check_vma=False
    )
```

```python
import functools

import jax
import jax.numpy as jnp
from jax import lax
from jax.experimental import pallas as pl
from jax.experimental.pallas import tpu as pltpu
from jax.sharding import PartitionSpec as P

MESH = pl.DeviceIdType.MESH

FULL = 1024
HALF = 512
SLICE = 64
DEPTH = 1280
BLOCK = 256
BLOCKS = 8
PIECES = 8
WHEN = (
    (0, 3, 5, 8, 11, 14, 16, 19),
    (1, 4, 8, 9, 12, 15, 17, 20),
    (2, 7, 12, 13, 15, 19, 21, 23),
    (4, 10, 22, 16, 18, 24, 25, 30),
    (5, 14, 23, 19, 22, 28, 27, 31),
    (9, 17, 30, 23, 26, 32, 33, 35),
    (13, 22, 35, 27, 34, 36, 37, 38),
    (24, 29, 35, 28, 34, 37, 38, 39),
)
SEND_ON = (3, 5, 6, 7, 8, 11)


def code(v):
    return (v * jnp.abs(v) * (v * v)).astype(jnp.bfloat16)


def decode(b):
    b = b.astype(jnp.float32)
    m = jnp.maximum(jnp.abs(b), 1e-36)
    m = m * lax.rsqrt(m)
    m = m * lax.rsqrt(m)
    return jnp.where(b < 0, -m, m)


def kernel(
    r_hbm, s_hbm, c_hbm, g_ref, res_ref,
    r_ref, sall, cpad, cmd_t, acc, csend, crecv, near_s, near_r, far_s, far_r, sum_s, sum_r,
    xsend, xrecv, rall, turned,
    in_sem, s_ss, s_rs, ss, rs,
):
    row, col = lax.axis_index("row"), lax.axis_index("col")
    y, xh = row // 2, row % 2
    z, xl, core = col // 4, (col // 2) % 2, col % 2
    quad = xl * 2 + core
    y_up = (((y + 1) % 4) * 2 + xh, col)
    y_dn = (((y + 3) % 4) * 2 + xh, col)
    x_far = (y * 2 + 1 - xh, col)
    z_up = (row, ((z + 1) % 8) * 4 + quad)
    z_dn = (row, ((z + 7) % 8) * 4 + quad)
    z_up2 = (row, ((z + 2) % 8) * 4 + quad)
    z_dn2 = (row, ((z + 6) % 8) * 4 + quad)
    x_near = (row, z * 4 + (1 - xl) * 2 + core)
    twin = (row, z * 4 + xl * 2 + 1 - core)

    barrier = pltpu.get_barrier_semaphore()
    for device in (y_up, y_dn, x_far, z_up, z_dn, z_up2, z_dn2, x_near, twin):
        pl.semaphore_signal(barrier, inc=1, device_id=device, device_id_type=MESH)

    s_in = pltpu.make_async_copy(s_hbm, sall.at[0], in_sem.at[0])
    r_in = pltpu.make_async_copy(r_hbm, r_ref, in_sem.at[1])
    s_in.start()
    r_in.start()
    cpad[...] = jnp.zeros_like(cpad)
    def remote(src, dst, send, recv, device):
        return pltpu.make_async_remote_copy(
            src_ref=src, dst_ref=dst, send_sem=send, recv_sem=recv,
            device_id=device, device_id_type=MESH,
        )

    mid = DEPTH // 2
    lo, hi, every = pl.ds(0, mid), pl.ds(mid, mid), pl.ds(0, DEPTH)
    most, rest = pl.ds(0, 3 * DEPTH // 4), pl.ds(3 * DEPTH // 4, DEPTH // 4)
    left, right = pl.ds(0, 128), pl.ds(128, 128)
    s_moves = [
        remote(
            s_hbm.at[r0, c0] if i == 0 else sall.at[i, r0, c0],
            sall.at[j, r0, c1], s_ss.at[n], s_rs.at[n], device,
        )
        for n, (i, j, r0, c0, c1, device) in enumerate((
            (0, 1, every, left, left, y_up),
            (0, 1, every, left, right, y_dn),
            (0, 2, every, right, left, y_up),
            (0, 2, every, right, right, y_dn),
            (0, 3, every, left, left, x_far),
            (0, 3, every, right, right, x_far),
            (1, 4, lo, left, left, y_up),
            (1, 4, hi, right, left, y_dn),
            (2, 4, lo, left, right, y_up),
            (2, 4, hi, right, right, y_dn),
            (3, 5, every, left, left, y_up),
            (3, 5, every, left, right, y_dn),
            (3, 6, most, right, left, y_up),
            (3, 6, most, right, right, y_dn),
            (4, 7, every, left, left, x_far),
            (4, 7, every, right, right, x_far),
            (2, 6, rest, left, left, x_far),
            (2, 6, rest, right, right, x_far),
        ))
    ]
    passes = [
        ((0, 1), (6, 7)), ((2, 3), (8, 9, 16, 17)), ((4,), (10, 11)), ((5,), (12, 13)), ((6, 7), (14,)),
        ((8, 9), (15,)),
    ]
    dy = (z // 2 + 4 - y) % 4
    dx = (z % 2 + 2 - xh) % 2
    beside = (dy == 1) | (dy == 3)
    my_slot = jnp.where(beside, 1 + 4 * dx + xl, jnp.where(dy == 0, 3 * dx, 4 + 3 * dx))
    my_half = jnp.where(beside, (dy == 1).astype(jnp.int32), xl)
    c_in = pltpu.make_async_copy(
        c_hbm,
        cpad.at[pl.ds(pl.multiple_of(my_half * 128 + core * 64, 64), 64)],
        in_sem.at[2],
    )
    c_in.start()
    pl.semaphore_wait(barrier, 9)
    for i in (0, 1, 4, 2, 3, 5):
        s_moves[i].start()
    s_in.wait()

    c_in.wait()
    cmd_t[...] = cpad[...].T
    g_ref[...] = jnp.zeros_like(g_ref)
    r_in.wait()

    own0 = core * HALF
    other0 = (1 - core) * HALF

    def rows(start, size):
        return pl.ds(pl.multiple_of(start, size), size)

    def part(at, size=SLICE, skip=0):
        return rows(((z + at + 8) % 8) * SLICE + skip, size)

    def full_part(at, size=SLICE, skip=0):
        return rows(own0 + ((z + at + 8) % 8) * SLICE + skip, size)

    def core_move(g):
        return remote(csend.at[g], crecv.at[g], ss.at[g, 0], rs.at[g, 0], twin)

    one, two = (z_up, z_dn), (z_up2, z_dn2)

    def near_move(g, d):
        return remote(near_s.at[g, d], near_r.at[g, d], ss.at[g, 1 + d], rs.at[g, 1 + d], one[d])

    def far_move(g, d):
        return remote(far_s.at[g, d], far_r.at[g, d], ss.at[g, 3 + d], rs.at[g, 3 + d], two[d])

    def sum_move(g, d):
        return remote(sum_s.at[g, d], sum_r.at[g, d], ss.at[g, 5 + d], rs.at[g, 5 + d], two[d])

    def x_move(g):
        return remote(xsend.at[g], xrecv.at[g], ss.at[g, 7], rs.at[g, 7], x_near)

    def spread(g, d, n, at, device, size=SLICE, skip=0):
        here = rall.at[g, full_part(at, size, skip)]
        return remote(here, here, ss.at[g, n + d], rs.at[g, n + d], device)

    def out_1(g, d):
        return spread(g, d, 8, 0, one[d])

    def in_1(g, d):
        return spread(g, d, 8, (-1, 1)[d], one[d])

    def out_2(g, d):
        return spread(g, d, 10, 0, two[d])

    def in_2(g, d):
        return spread(g, d, 10, (-2, 2)[d], two[d])

    def out_3(g, d):
        return spread(g, d, 12, (-2, 2)[d], one[d])

    def in_3(g, d):
        return spread(g, d, 12, (-3, 3)[d], one[d])

    def out_4(g, d):
        return spread(g, d, 14, (-2, 2)[d], two[d], SLICE // 2, d * SLICE // 2)

    def in_4(g, d):
        return spread(g, d, 14, 4, two[d], SLICE // 2, d * SLICE // 2)

    def out_core(g):
        here = rall.at[g, rows(own0, HALF)]
        return remote(here, here, ss.at[g, 16], rs.at[g, 16], twin)

    def in_core(g):
        here = rall.at[g, rows(other0, HALF)]
        return remote(here, here, ss.at[g, 16], rs.at[g, 16], twin)

    def both(g, at, size=SLICE, skip=0):
        here = part(at, size, skip)
        return acc[g, here, :] + decode(crecv[g, here, :])

    def pass_on(n):
        arrived, onward = passes[n]
        for i in arrived:
            s_moves[i].wait_recv()
        for i in onward:
            s_moves[i].start()

    def stage_predict(g):
        for slot in (5, 6, 7):

            @pl.when(g == slot)
            def _(slot=slot):
                s_moves[2 * slot].wait_recv()
                s_moves[2 * slot + 1].wait_recv()
                if slot == 6:
                    s_moves[16].wait_recv()
                    s_moves[17].wait_recv()

        mine = (g == my_slot).astype(jnp.float32)
        tile = 512

        def predicted(start):
            p = jnp.dot(
                r_ref[rows(start, tile), :], sall[g], preferred_element_type=jnp.float32
            )
            return p - cmd_t[rows(start, tile), :] * mine

        @pl.loop(0, HALF // tile)
        def _(i):
            csend[g, rows(i * tile, tile), :] = code(predicted(other0 + i * tile))

        core_move(g).start()

        @pl.loop(0, HALF // tile)
        def _(i):
            acc[g, rows(i * tile, tile), :] = predicted(own0 + i * tile)

    half = SLICE // 2
    first, second = pl.ds(0, SLICE), pl.ds(SLICE, SLICE)

    def stage_1(g):
        core_move(g).wait_recv()
        for d, sign in ((0, 1), (1, -1)):
            far_s[g, d] = code(both(g, 4, half, d * half))
            far_move(g, d).start()
            near_s[g, d, second, :] = code(both(g, 3 * sign))
            near_s[g, d, first, :] = code(both(g, sign))
            near_move(g, d).start()

    def stage_2(g):
        for d, sign in ((0, 1), (1, -1)):
            near_move(g, d).wait_recv()
            far_move(g, d).wait_recv()
            for h in (0, 1):
                total = both(g, 2 * sign, half, h * half) + decode(
                    near_r[g, d, pl.ds(SLICE + h * half, half), :]
                )
                if h == d:
                    total = total + decode(far_r[g, d])
                sum_s[g, d, pl.ds(h * half, half), :] = code(total)
            sum_move(g, d).start()

    def stage_3(g):
        total = both(g, 0) + decode(near_r[g, 0, first, :]) + decode(near_r[g, 1, first, :])
        for d in (0, 1):
            sum_move(g, d).wait_recv()
            total = total + decode(sum_r[g, d])
        acc[g, part(0), :] = total
        xsend[g] = code(total)
        x_move(g).start()

    def stage_4(g):
        x_move(g).wait_recv()
        low = (acc[g, part(0), :] + decode(xrecv[g])).astype(jnp.bfloat16)
        rall[g, full_part(0), :] = low
        for d in (0, 1):
            out_2(g, d).start()
        for d in (0, 1):
            out_1(g, d).start()

    def stage_5(g):
        for d in (0, 1):
            in_2(g, d).wait_recv()
            out_4(g, d).start()
            out_3(g, d).start()

    scale_factor = 1.0 / jnp.sqrt(jnp.float32(2048))

    def add_gradient(g, start, when):
        here = rows(start, HALF)
        added = g_ref[here, :] + lax.dot_general(
            rall[g, here, :], sall[g], (((1,), (1,)), ((), ())),
            preferred_element_type=jnp.float32,
        )
        g_ref[here, :] = added * jnp.where(g == when.index(max(when)), scale_factor, 1.0)

    def stage_6(g):
        for d in (0, 1):
            in_1(g, d).wait_recv()
            in_3(g, d).wait_recv()
            in_4(g, d).wait_recv()
        out_core(g).start()
        add_gradient(g, own0, WHEN[6])

    def stage_gradient(g):
        in_core(g).wait_recv()
        add_gradient(g, other0, WHEN[7])

        @pl.when(g == my_slot)
        def _():
            half = rall[g, :, pl.ds(pl.multiple_of(my_half * 128, 128), 128)]
            turned[...] = half.astype(jnp.float32).T
            res_ref[...] = turned[rows(core * 64, 64), :]

        core_move(g).wait_send()
        for move in (near_move, far_move, sum_move, out_1, out_2, out_3, out_4):
            for d in (0, 1):
                move(g, d).wait_send()
        x_move(g).wait_send()
        out_core(g).wait_send()

    stages = [
        stage_predict, stage_1, stage_2, stage_3, stage_4, stage_5, stage_6, stage_gradient,
    ]
    order = [6, 5, 4, 3, 2, 1, 0, 7]

    def tick(t, carry):
        for n, at in enumerate(SEND_ON):
            pl.when(t == at)(functools.partial(pass_on, n))
        for k in order:
            g, active = jnp.int32(0), t == WHEN[k][0]
            for i in range(1, BLOCKS):
                g = jnp.where(t == WHEN[k][i], i, g)
                active = active | (t == WHEN[k][i])

            @pl.when(active)
            def _(k=k, g=g):
                stages[k](g)

        return carry

    lax.fori_loop(0, max(WHEN[-1]) + 1, tick, 0)
    for move in s_moves:
        move.wait_send()


def finish(g_ref, res_ref, g_hbm, res_hbm, sem):
    size = FULL // PIECES
    moves = [pltpu.make_async_copy(res_ref, res_hbm, sem.at[PIECES])]
    for i in range(PIECES):
        here = pl.ds(i * size, size)
        moves.append(pltpu.make_async_copy(g_ref.at[here], g_hbm.at[here], sem.at[i]))
    for move in moves:
        move.start()
    for move in moves:
        move.wait()


def on_device(reconstructor, slopes, commands):
    vmem = pltpu.VMEM
    gradient, residual = pl.pallas_call(
        kernel,
        out_shape=(
            pltpu.VMEM((FULL, DEPTH), jnp.float32),
            pltpu.VMEM((64, FULL), jnp.float32),
        ),
        in_specs=[pl.BlockSpec(memory_space=pl.ANY)] * 3,
        out_specs=[pl.BlockSpec(memory_space=pltpu.VMEM)] * 2,
        scratch_shapes=[
            vmem((FULL, DEPTH), jnp.bfloat16),
            vmem((BLOCKS, DEPTH, BLOCK), jnp.bfloat16),
            vmem((BLOCK, FULL), jnp.float32),
            vmem((FULL, BLOCK), jnp.float32),
            vmem((BLOCKS, HALF, BLOCK), jnp.float32),
            vmem((BLOCKS, HALF, BLOCK), jnp.bfloat16),
            vmem((BLOCKS, HALF, BLOCK), jnp.bfloat16),
            vmem((BLOCKS, 2, 2 * SLICE, BLOCK), jnp.bfloat16),
            vmem((BLOCKS, 2, 2 * SLICE, BLOCK), jnp.bfloat16),
            vmem((BLOCKS, 2, SLICE // 2, BLOCK), jnp.bfloat16),
            vmem((BLOCKS, 2, SLICE // 2, BLOCK), jnp.bfloat16),
            vmem((BLOCKS, 2, SLICE, BLOCK), jnp.bfloat16),
            vmem((BLOCKS, 2, SLICE, BLOCK), jnp.bfloat16),
            vmem((BLOCKS, SLICE, BLOCK), jnp.bfloat16),
            vmem((BLOCKS, SLICE, BLOCK), jnp.bfloat16),
            vmem((BLOCKS, FULL, BLOCK), jnp.bfloat16),
            vmem((128, FULL), jnp.float32),
            pltpu.SemaphoreType.DMA((3,)),
            pltpu.SemaphoreType.DMA((18,)),
            pltpu.SemaphoreType.DMA((18,)),
            pltpu.SemaphoreType.DMA((BLOCKS, 17)),
            pltpu.SemaphoreType.DMA((BLOCKS, 17)),
        ],
        compiler_params=pltpu.CompilerParams(
            collective_id=0, has_side_effects=True, vmem_limit_bytes=56 << 20
        ),
        cost_estimate=pl.CostEstimate(
            flops=4 * 2048 * FULL * DEPTH, bytes_accessed=9 << 20, transcendentals=0
        ),
    )(reconstructor, slopes, commands)
    return pl.pallas_call(
        finish,
        out_shape=(
            jax.ShapeDtypeStruct((FULL, DEPTH), jnp.float32),
            jax.ShapeDtypeStruct((64, FULL), jnp.float32),
        ),
        in_specs=[pl.BlockSpec(memory_space=pltpu.VMEM)] * 2,
        out_specs=[pl.BlockSpec(memory_space=pl.ANY)] * 2,
        scratch_shapes=[
            pltpu.SemaphoreType.DMA((PIECES + 1,)),
        ],
        compiler_params=pltpu.CompilerParams(vmem_limit_bytes=4 << 20),
    )(gradient, residual)


def solution(mesh):
    in_specs = (P("row", "col"), P("col", "row"), P("col", "row"))
    out_specs = (P("row", "col"), P("col", "row"))
    return jax.shard_map(
        on_device, mesh=mesh, in_specs=in_specs, out_specs=out_specs, check_vma=False
    )
```

```python
import functools

import jax
import jax.numpy as jnp
from jax import lax
from jax.experimental import pallas as pl
from jax.experimental.pallas import tpu as pltpu
from jax.sharding import PartitionSpec as P

MESH = pl.DeviceIdType.MESH

FULL = 1024
HALF = 512
SLICE = 64
DEPTH = 1280
BLOCK = 256
BLOCKS = 8
PIECES = 8
KINDS = {
    "two": (0, 7,),
    "xf": (1, 6,),
    "ring": (2, 3, 4, 5,),
}
ORDER = (
    ("predict", 0), ("two_1", 0), ("two_2", 0), ("pass_on", 0), ("predict", 1), ("xf_1", 1),
    ("two_3", 0), ("pass_on", 1), ("predict", 2), ("pass_on", 2), ("pass_on", 3), ("predict", 3),
    ("ring_1", 2), ("pass_on", 4), ("ring_1", 3), ("xf_2", 1), ("ring_2", 2), ("two_4", 0),
    ("pass_on", 5), ("predict", 4), ("ring_1", 4), ("ring_3", 2), ("ring_2", 3), ("xf_3", 1),
    ("two_5", 0), ("ring_2", 4), ("ring_4", 2), ("ring_3", 3), ("predict", 5), ("ring_1", 5),
    ("ring_5", 2), ("ring_3", 4), ("xf_4", 1), ("ring_4", 3), ("predict", 6), ("ring_2", 5),
    ("ring_4", 4), ("xf_1", 6), ("ring_6", 2), ("xf_5", 1), ("predict", 7), ("ring_3", 5),
    ("two_1", 7), ("ring_5", 4), ("ring_7", 2), ("ring_5", 3), ("ring_4", 5), ("xf_2", 6),
    ("xf_6", 1), ("ring_6", 4), ("ring_6", 3), ("two_2", 7), ("ring_8", 2), ("two_6", 0),
    ("ring_5", 5), ("xf_3", 6), ("ring_7", 4), ("ring_7", 3), ("xf_7", 1), ("ring_6", 5),
    ("ring_9", 2), ("gradient", 1), ("xf_4", 6), ("ring_8", 4), ("two_3", 7), ("ring_8", 3),
    ("ring_7", 5), ("ring_10", 2), ("xf_5", 6), ("two_4", 7), ("ring_9", 4), ("ring_9", 3),
    ("gradient", 0), ("ring_8", 5), ("gradient", 2), ("xf_6", 6), ("two_5", 7), ("ring_10", 4),
    ("ring_10", 3), ("ring_9", 5), ("gradient", 4), ("gradient", 3), ("xf_7", 6), ("two_6", 7),
    ("ring_10", 5), ("gradient", 6), ("gradient", 7), ("gradient", 5),
)
LAST_OWN, LAST_OTHER = 5, 5


def code(v):
    return (v * jnp.abs(v) * (v * v)).astype(jnp.bfloat16)


def decode(b):
    b = b.astype(jnp.float32)
    m = jnp.maximum(jnp.abs(b), 1e-36)
    m = m * lax.rsqrt(m)
    m = m * lax.rsqrt(m)
    return jnp.where(b < 0, -m, m)


def kernel(
    r_hbm, s_hbm, c_hbm, g_ref, res_ref,
    r_ref, sall, cpad, cmd_t, acc, csend, crecv, near_s, near_r, far_s, far_r, sum_s, sum_r,
    ring_s, ring_r, xsend, xrecv, rall, turned,
    in_sem, s_ss, s_rs, ss, rs,
):
    row, col = lax.axis_index("row"), lax.axis_index("col")
    y, xh = row // 2, row % 2
    z, xl, core = col // 4, (col // 2) % 2, col % 2
    quad = xl * 2 + core
    y_up = (((y + 1) % 4) * 2 + xh, col)
    y_dn = (((y + 3) % 4) * 2 + xh, col)
    x_far = (y * 2 + 1 - xh, col)
    z_up = (row, ((z + 1) % 8) * 4 + quad)
    z_dn = (row, ((z + 7) % 8) * 4 + quad)
    z_up2 = (row, ((z + 2) % 8) * 4 + quad)
    z_dn2 = (row, ((z + 6) % 8) * 4 + quad)
    x_near = (row, z * 4 + (1 - xl) * 2 + core)
    twin = (row, z * 4 + xl * 2 + 1 - core)

    barrier = pltpu.get_barrier_semaphore()
    for device in (y_up, y_dn, x_far, z_up, z_dn, z_up2, z_dn2, x_near, twin):
        pl.semaphore_signal(barrier, inc=1, device_id=device, device_id_type=MESH)

    s_in = pltpu.make_async_copy(s_hbm, sall.at[0], in_sem.at[0])
    r_in = pltpu.make_async_copy(r_hbm, r_ref, in_sem.at[1])
    s_in.start()
    r_in.start()
    cpad[...] = jnp.zeros_like(cpad)
    def remote(src, dst, send, recv, device):
        return pltpu.make_async_remote_copy(
            src_ref=src, dst_ref=dst, send_sem=send, recv_sem=recv,
            device_id=device, device_id_type=MESH,
        )

    mid = DEPTH // 2
    lo, hi, every = pl.ds(0, mid), pl.ds(mid, mid), pl.ds(0, DEPTH)
    most, rest = pl.ds(0, 3 * DEPTH // 4), pl.ds(3 * DEPTH // 4, DEPTH // 4)
    left, right = pl.ds(0, 128), pl.ds(128, 128)
    s_moves = [
        remote(
            s_hbm.at[r0, c0] if i == 0 else sall.at[i, r0, c0],
            sall.at[j, r0, c1], s_ss.at[n], s_rs.at[n], device,
        )
        for n, (i, j, r0, c0, c1, device) in enumerate((
            (0, 1, every, left, left, y_up),
            (0, 1, every, left, right, y_dn),
            (0, 2, every, right, left, y_up),
            (0, 2, every, right, right, y_dn),
            (0, 3, every, left, left, x_far),
            (0, 3, every, right, right, x_far),
            (1, 4, lo, left, left, y_up),
            (1, 4, hi, right, left, y_dn),
            (2, 4, lo, left, right, y_up),
            (2, 4, hi, right, right, y_dn),
            (3, 5, every, left, left, y_up),
            (3, 5, every, left, right, y_dn),
            (3, 6, most, right, left, y_up),
            (3, 6, most, right, right, y_dn),
            (4, 7, every, left, left, x_far),
            (4, 7, every, right, right, x_far),
            (2, 6, rest, left, left, x_far),
            (2, 6, rest, right, right, x_far),
        ))
    ]
    passes = [
        ((0, 1), (6, 7)), ((2, 3), (8, 9, 16, 17)), ((4,), (10, 11)), ((5,), (12, 13)), ((6, 7), (14,)),
        ((8, 9), (15,)),
    ]
    dy = (z // 2 + 4 - y) % 4
    dx = (z % 2 + 2 - xh) % 2
    beside = (dy == 1) | (dy == 3)
    my_slot = jnp.where(beside, 1 + 4 * dx + xl, jnp.where(dy == 0, 3 * dx, 4 + 3 * dx))
    my_half = jnp.where(beside, (dy == 1).astype(jnp.int32), xl)
    c_in = pltpu.make_async_copy(
        c_hbm,
        cpad.at[pl.ds(pl.multiple_of(my_half * 128 + core * 64, 64), 64)],
        in_sem.at[2],
    )
    c_in.start()
    pl.semaphore_wait(barrier, 9)
    for i in (0, 1, 4, 2, 3, 5):
        s_moves[i].start()
    s_in.wait()

    c_in.wait()
    cmd_t[...] = cpad[...].T
    g_ref[...] = jnp.zeros_like(g_ref)
    r_in.wait()

    own0 = core * HALF
    other0 = (1 - core) * HALF

    def rows(start, size):
        return pl.ds(pl.multiple_of(start, size), size)

    def core_move(g):
        return remote(csend.at[g], crecv.at[g], ss.at[g, 0], rs.at[g, 0], twin)

    one, two = (z_up, z_dn), (z_up2, z_dn2)

    def out_core(g):
        here = rall.at[g, rows(own0, HALF)]
        return remote(here, here, ss.at[g, 16], rs.at[g, 16], twin)

    def in_core(g):
        here = rall.at[g, rows(other0, HALF)]
        return remote(here, here, ss.at[g, 16], rs.at[g, 16], twin)

    def pass_on(n):
        arrived, onward = passes[n]
        for i in arrived:
            s_moves[i].wait_recv()
        for i in onward:
            s_moves[i].start()

    def stage_predict(g):
        if g >= 5:
            s_moves[2 * g].wait_recv()
            s_moves[2 * g + 1].wait_recv()
        if g == 6:
            s_moves[16].wait_recv()
            s_moves[17].wait_recv()

        mine = (g == my_slot).astype(jnp.float32)
        tile = 512

        def predicted(start):
            p = jnp.dot(
                r_ref[rows(start, tile), :], sall[g], preferred_element_type=jnp.float32
            )
            return p - cmd_t[rows(start, tile), :] * mine

        @pl.loop(0, HALF // tile)
        def _(i):
            csend[g, rows(i * tile, tile), :] = code(predicted(other0 + i * tile))

        core_move(g).start()

        @pl.loop(0, HALF // tile)
        def _(i):
            acc[g, rows(i * tile, tile), :] = predicted(own0 + i * tile)

    scale_factor = 1.0 / jnp.sqrt(jnp.float32(2048))

    def add_gradient(g, start, last):
        here = rows(start, HALF)
        added = g_ref[here, :] + lax.dot_general(
            rall[g, here, :], sall[g], (((1,), (1,)), ((), ())),
            preferred_element_type=jnp.float32,
        )
        g_ref[here, :] = added * scale_factor if g == last else added

    def share(g):
        out_core(g).start()
        add_gradient(g, own0, LAST_OWN)

    def with_twin(g, here):
        return acc[g, here, :] + decode(crecv[g, here, :])

    def tree(size, base, term):
        half = size // 2
        first, second = pl.ds(0, size), pl.ds(size, size)

        def part(at, count=size, skip=0):
            return rows(base + ((z + at + 8) % 8) * size + skip, count)

        def near_move(g, d):
            here = near_s.at[g, d, pl.ds(0, 2 * size)]
            there = near_r.at[g, d, pl.ds(0, 2 * size)]
            return remote(here, there, ss.at[g, 1 + d], rs.at[g, 1 + d], one[d])

        def far_move(g, d):
            here, there = far_s.at[g, d, pl.ds(0, half)], far_r.at[g, d, pl.ds(0, half)]
            return remote(here, there, ss.at[g, 3 + d], rs.at[g, 3 + d], two[d])

        def sum_move(g, d):
            here, there = sum_s.at[g, d, first], sum_r.at[g, d, first]
            return remote(here, there, ss.at[g, 5 + d], rs.at[g, 5 + d], two[d])

        def spread(g, d, n, at, device, count=size, skip=0):
            start = own0 + base + ((z + at + 8) % 8) * size + skip
            here = rall.at[g, rows(start, count)]
            return remote(here, here, ss.at[g, n + d], rs.at[g, n + d], device)

        def out_1(g, d):
            return spread(g, d, 8, 0, one[d])

        def in_1(g, d):
            return spread(g, d, 8, (-1, 1)[d], one[d])

        def out_2(g, d):
            return spread(g, d, 10, 0, two[d])

        def in_2(g, d):
            return spread(g, d, 10, (-2, 2)[d], two[d])

        def out_3(g, d):
            return spread(g, d, 12, (-2, 2)[d], one[d])

        def in_3(g, d):
            return spread(g, d, 12, (-3, 3)[d], one[d])

        def out_4(g, d):
            return spread(g, d, 14, (-2, 2)[d], two[d], half, d * half)

        def in_4(g, d):
            return spread(g, d, 14, 4, two[d], half, d * half)

        def send_terms(g):
            for d, sign in ((0, 1), (1, -1)):
                far_s[g, d, pl.ds(0, half), :] = code(term(g, part(4, half, d * half)))
                far_move(g, d).start()
                near_s[g, d, second, :] = code(term(g, part(3 * sign)))
                near_s[g, d, first, :] = code(term(g, part(sign)))
                near_move(g, d).start()

        def send_sums(g):
            for d, sign in ((0, 1), (1, -1)):
                near_move(g, d).wait_recv()
                far_move(g, d).wait_recv()
                for h in (0, 1):
                    total = term(g, part(2 * sign, half, h * half)) + decode(
                        near_r[g, d, pl.ds(size + h * half, half), :]
                    )
                    if h == d:
                        total = total + decode(far_r[g, d, pl.ds(0, half), :])
                    sum_s[g, d, pl.ds(h * half, half), :] = code(total)
                sum_move(g, d).start()

        def total(g):
            total = term(g, part(0))
            for d in (0, 1):
                sum_move(g, d).wait_recv()
                total = total + decode(near_r[g, d, first, :]) + decode(sum_r[g, d, first, :])
            return total

        def hand_round(g, residual):
            rall[g, rows(own0 + base + z * size, size), :] = residual.astype(jnp.bfloat16)
            for d in (0, 1):
                out_2(g, d).start()
            for d in (0, 1):
                out_1(g, d).start()

        def hand_on(g):
            for d in (0, 1):
                in_2(g, d).wait_recv()
                out_4(g, d).start()
                out_3(g, d).start()

        def all_here(g):
            for d in (0, 1):
                in_1(g, d).wait_recv()
                in_3(g, d).wait_recv()
                in_4(g, d).wait_recv()

        def sent(g):
            for move in (near_move, far_move, sum_move, out_1, out_2, out_3, out_4):
                for d in (0, 1):
                    move(g, d).wait_send()

        return part, send_terms, send_sums, total, hand_round, hand_on, all_here, sent

    def x_move(g):
        here, there = xsend.at[g, pl.ds(0, SLICE)], xrecv.at[g, pl.ds(0, SLICE)]
        return remote(here, there, ss.at[g, 18], rs.at[g, 18], x_near)

    (
        two_part, two_terms, two_sums, two_total, two_round, two_on, two_here, two_sent,
    ) = tree(SLICE, 0, with_twin)

    def two_1(g):
        core_move(g).wait_recv()
        two_terms(g)

    def two_3(g):
        total = two_total(g)
        acc[g, two_part(0), :] = total
        xsend[g, pl.ds(0, SLICE), :] = code(total)
        x_move(g).start()

    def two_4(g):
        x_move(g).wait_recv()
        two_round(g, acc[g, two_part(0), :] + decode(xrecv[g, pl.ds(0, SLICE), :]))

    def two_6(g):
        two_here(g)
        share(g)

    quarter = HALF // 2

    def half_move(g):
        return remote(xsend.at[g], xrecv.at[g], ss.at[g, 7], rs.at[g, 7], x_near)

    def out_x(g):
        here = rall.at[g, rows(own0 + xl * quarter, quarter)]
        return remote(here, here, ss.at[g, 17], rs.at[g, 17], x_near)

    def in_x(g):
        here = rall.at[g, rows(own0 + (1 - xl) * quarter, quarter)]
        return remote(here, here, ss.at[g, 17], rs.at[g, 17], x_near)

    xf_part, xf_terms, xf_sums, xf_total, xf_round, xf_on, xf_here, xf_sent = tree(
        SLICE // 2, xl * quarter, lambda g, here: acc[g, here, :]
    )

    def xf_1(g):
        core_move(g).wait_recv()

        @pl.loop(0, quarter // SLICE)
        def _(i):
            here = rows((1 - xl) * quarter + i * SLICE, SLICE)
            xsend[g, rows(i * SLICE, SLICE), :] = code(with_twin(g, here))

        half_move(g).start()

    def xf_2(g):
        half_move(g).wait_recv()

        @pl.loop(0, quarter // SLICE)
        def _(i):
            here = rows(xl * quarter + i * SLICE, SLICE)
            other = decode(xrecv[g, rows(i * SLICE, SLICE), :])
            acc[g, here, :] = with_twin(g, here) + other

        xf_terms(g)

    def xf_4(g):
        xf_round(g, xf_total(g))

    def xf_6(g):
        xf_here(g)
        out_x(g).start()

    def xf_7(g):
        in_x(g).wait_recv()
        share(g)

    def ring_part(at):
        return rows(((z + at + 8) % 8) * SLICE, SLICE)

    def ring_here(g, at):
        return rall.at[g, rows(own0 + ((z + at + 8) % 8) * SLICE, SLICE)]

    def up_move(g, i):
        return remote(ring_s.at[g, i], ring_r.at[g, i], ss.at[g, 1 + i], rs.at[g, 1 + i], z_up)

    def dn_move(g, i):
        return remote(
            ring_s.at[g, 4 + i], ring_r.at[g, 4 + i], ss.at[g, 5 + i], rs.at[g, 5 + i], z_dn
        )

    def out_up(g, i):
        here = ring_here(g, -i)
        return remote(here, here, ss.at[g, 9 + i], rs.at[g, 9 + i], z_up)

    def in_up(g, i):
        here = ring_here(g, -i - 1)
        return remote(here, here, ss.at[g, 9 + i], rs.at[g, 9 + i], z_up)

    def out_dn(g, i):
        here = ring_here(g, i)
        return remote(here, here, ss.at[g, 12 + i], rs.at[g, 12 + i], z_dn)

    def in_dn(g, i):
        here = ring_here(g, i + 1)
        return remote(here, here, ss.at[g, 12 + i], rs.at[g, 12 + i], z_dn)

    def send_up(g, i):
        total = with_twin(g, ring_part(4 - i))
        if i:
            up_move(g, i - 1).wait_recv()
            total = total + decode(ring_r[g, i - 1])
        ring_s[g, i] = code(total)
        up_move(g, i).start()

    def send_dn(g, i):
        total = with_twin(g, ring_part(i - 3))
        if i:
            dn_move(g, i - 1).wait_recv()
            total = total + decode(ring_r[g, 3 + i])
        ring_s[g, 4 + i] = code(total)
        dn_move(g, i).start()

    def ring_1(g):
        core_move(g).wait_recv()
        send_up(g, 0)

    def ring_2(g, i=1):
        send_dn(g, i - 1)
        send_up(g, i)

    def ring_5(g):
        dn_move(g, 2).wait_recv()
        up_move(g, 3).wait_recv()
        total = with_twin(g, ring_part(0)) + decode(ring_r[g, 6]) + decode(ring_r[g, 3])
        acc[g, ring_part(0), :] = total
        xsend[g, pl.ds(0, SLICE), :] = code(total)
        x_move(g).start()

    def ring_6(g):
        x_move(g).wait_recv()
        low = acc[g, ring_part(0), :] + decode(xrecv[g, pl.ds(0, SLICE), :])
        rall[g, rows(own0 + z * SLICE, SLICE), :] = low.astype(jnp.bfloat16)
        out_dn(g, 0).start()
        out_up(g, 0).start()

    def ring_7(g, i=0):
        in_dn(g, i).wait_recv()
        out_dn(g, i + 1).start()
        in_up(g, i).wait_recv()
        out_up(g, i + 1).start()

    def ring_9(g):
        in_dn(g, 2).wait_recv()
        out_dn(g, 3).start()
        in_up(g, 2).wait_recv()

    def ring_10(g):
        in_dn(g, 3).wait_recv()
        share(g)

    def ring_sent(g):
        for i in range(4):
            up_move(g, i).wait_send()
            out_dn(g, i).wait_send()
        for i in range(3):
            dn_move(g, i).wait_send()
            out_up(g, i).wait_send()

    def stage_gradient(g):
        in_core(g).wait_recv()
        add_gradient(g, other0, LAST_OTHER)

        @pl.when(g == my_slot)
        def _():
            half = rall[g, :, pl.ds(pl.multiple_of(my_half * 128, 128), 128)]
            turned[...] = half.astype(jnp.float32).T
            res_ref[...] = turned[rows(core * 64, 64), :]

        core_move(g).wait_send()
        out_core(g).wait_send()

        if g in KINDS["two"]:
            two_sent(g)
            x_move(g).wait_send()

        if g in KINDS["xf"]:
            xf_sent(g)
            half_move(g).wait_send()
            out_x(g).wait_send()

        if g in KINDS["ring"]:
            ring_sent(g)
            x_move(g).wait_send()

    stages = {
        "pass_on": pass_on, "predict": stage_predict, "gradient": stage_gradient,
        "two_1": two_1, "two_2": two_sums, "two_3": two_3, "two_4": two_4, "two_5": two_on,
        "two_6": two_6,
        "xf_1": xf_1, "xf_2": xf_2, "xf_3": xf_sums, "xf_4": xf_4, "xf_5": xf_on, "xf_6": xf_6,
        "xf_7": xf_7,
        "ring_1": ring_1, "ring_2": ring_2, "ring_3": functools.partial(ring_2, i=2),
        "ring_4": functools.partial(ring_2, i=3), "ring_5": ring_5, "ring_6": ring_6,
        "ring_7": ring_7, "ring_8": functools.partial(ring_7, i=1), "ring_9": ring_9,
        "ring_10": ring_10,
    }

    for name, g in ORDER:
        stages[name](g)

    for move in s_moves:
        move.wait_send()


def finish(g_ref, res_ref, g_hbm, res_hbm, sem):
    size = FULL // PIECES
    moves = [pltpu.make_async_copy(res_ref, res_hbm, sem.at[PIECES])]
    for i in range(PIECES):
        here = pl.ds(i * size, size)
        moves.append(pltpu.make_async_copy(g_ref.at[here], g_hbm.at[here], sem.at[i]))
    for move in moves:
        move.start()
    for move in moves:
        move.wait()


def on_device(reconstructor, slopes, commands):
    vmem = pltpu.VMEM
    gradient, residual = pl.pallas_call(
        kernel,
        out_shape=(
            pltpu.VMEM((FULL, DEPTH), jnp.float32),
            pltpu.VMEM((64, FULL), jnp.float32),
        ),
        in_specs=[pl.BlockSpec(memory_space=pl.ANY)] * 3,
        out_specs=[pl.BlockSpec(memory_space=pltpu.VMEM)] * 2,
        scratch_shapes=[
            vmem((FULL, DEPTH), jnp.bfloat16),
            vmem((BLOCKS, DEPTH, BLOCK), jnp.bfloat16),
            vmem((BLOCK, FULL), jnp.float32),
            vmem((FULL, BLOCK), jnp.float32),
            vmem((BLOCKS, HALF, BLOCK), jnp.float32),
            vmem((BLOCKS, HALF, BLOCK), jnp.bfloat16),
            vmem((BLOCKS, HALF, BLOCK), jnp.bfloat16),
            vmem((BLOCKS, 2, 2 * SLICE, BLOCK), jnp.bfloat16),
            vmem((BLOCKS, 2, 2 * SLICE, BLOCK), jnp.bfloat16),
            vmem((BLOCKS, 2, SLICE // 2, BLOCK), jnp.bfloat16),
            vmem((BLOCKS, 2, SLICE // 2, BLOCK), jnp.bfloat16),
            vmem((BLOCKS, 2, SLICE, BLOCK), jnp.bfloat16),
            vmem((BLOCKS, 2, SLICE, BLOCK), jnp.bfloat16),
            vmem((BLOCKS, 7, SLICE, BLOCK), jnp.bfloat16),
            vmem((BLOCKS, 7, SLICE, BLOCK), jnp.bfloat16),
            vmem((BLOCKS, HALF // 2, BLOCK), jnp.bfloat16),
            vmem((BLOCKS, HALF // 2, BLOCK), jnp.bfloat16),
            vmem((BLOCKS, FULL, BLOCK), jnp.bfloat16),
            vmem((128, FULL), jnp.float32),
            pltpu.SemaphoreType.DMA((3,)),
            pltpu.SemaphoreType.DMA((18,)),
            pltpu.SemaphoreType.DMA((18,)),
            pltpu.SemaphoreType.DMA((BLOCKS, 19)),
            pltpu.SemaphoreType.DMA((BLOCKS, 19)),
        ],
        compiler_params=pltpu.CompilerParams(
            collective_id=0, has_side_effects=True, vmem_limit_bytes=56 << 20
        ),
        cost_estimate=pl.CostEstimate(
            flops=4 * 2048 * FULL * DEPTH, bytes_accessed=9 << 20, transcendentals=0
        ),
    )(reconstructor, slopes, commands)
    return pl.pallas_call(
        finish,
        out_shape=(
            jax.ShapeDtypeStruct((FULL, DEPTH), jnp.float32),
            jax.ShapeDtypeStruct((64, FULL), jnp.float32),
        ),
        in_specs=[pl.BlockSpec(memory_space=pltpu.VMEM)] * 2,
        out_specs=[pl.BlockSpec(memory_space=pl.ANY)] * 2,
        scratch_shapes=[
            pltpu.SemaphoreType.DMA((PIECES + 1,)),
        ],
        compiler_params=pltpu.CompilerParams(vmem_limit_bytes=4 << 20),
    )(gradient, residual)


def solution(mesh):
    in_specs = (P("row", "col"), P("col", "row"), P("col", "row"))
    out_specs = (P("row", "col"), P("col", "row"))
    return jax.shard_map(
        on_device, mesh=mesh, in_specs=in_specs, out_specs=out_specs, check_vma=False
    )
```

```python
import functools

import jax
import jax.numpy as jnp
from jax import lax
from jax.experimental import pallas as pl
from jax.experimental.pallas import tpu as pltpu
from jax.sharding import PartitionSpec as P

MESH = pl.DeviceIdType.MESH

FULL = 1024
HALF = 512
SLICE = 64
DEPTH = 1280
BLOCK = 256
BLOCKS = 8
PIECES = 8
KINDS = {
    "two": (0, 7,),
    "xf": (1, 6,),
    "ring": (2, 3, 4, 5,),
}
ORDER = (
    ("predict", 0), ("two_1", 0), ("pass_on", 0), ("two_2", 0), ("predict", 1), ("xf_1", 1),
    ("pass_on", 1), ("pass_on", 2), ("pass_on", 3), ("predict", 2), ("two_3", 0), ("ring_1", 2),
    ("xf_2", 1), ("predict", 3), ("pass_on", 4), ("ring_2", 2), ("ring_1", 3), ("pass_on", 5),
    ("predict", 4), ("xf_3", 1), ("ring_1", 4), ("ring_3", 2), ("two_4", 0), ("ring_2", 3),
    ("ring_2", 4), ("ring_4", 2), ("xf_4", 1), ("predict", 5), ("ring_1", 5), ("ring_3", 3),
    ("ring_3", 4), ("two_5", 0), ("ring_5", 2), ("xf_5", 1), ("predict", 6), ("ring_2", 5),
    ("ring_4", 3), ("xf_1", 6), ("ring_4", 4), ("ring_6", 2), ("predict", 7), ("ring_3", 5),
    ("ring_5", 3), ("two_1", 7), ("ring_5", 4), ("xf_2", 6), ("ring_4", 5), ("xf_6", 1),
    ("ring_6", 4), ("ring_7", 2), ("ring_6", 3), ("xf_3", 6), ("ring_5", 5), ("two_2", 7),
    ("ring_7", 4), ("two_6", 0), ("ring_8", 2), ("xf_7", 1), ("ring_7", 3), ("xf_4", 6),
    ("ring_6", 5), ("gradient", 0), ("ring_8", 4), ("two_3", 7), ("ring_9", 2), ("ring_8", 3),
    ("xf_5", 6), ("gradient", 1), ("ring_7", 5), ("ring_9", 4), ("two_4", 7), ("ring_10", 2),
    ("xf_6", 6), ("ring_8", 5), ("gradient", 2), ("ring_9", 3), ("two_5", 7), ("ring_10", 4),
    ("ring_9", 5), ("gradient", 4), ("ring_10", 3), ("xf_7", 6), ("gradient", 3), ("two_6", 7),
    ("ring_10", 5), ("gradient", 6), ("gradient", 7), ("gradient", 5),
)
LAST_OWN, LAST_OTHER = 5, 5


def code(v):
    return (v * jnp.abs(v) * (v * v)).astype(jnp.bfloat16)


def decode(b):
    b = b.astype(jnp.float32)
    m = jnp.maximum(jnp.abs(b), 1e-36)
    m = m * lax.rsqrt(m)
    m = m * lax.rsqrt(m)
    return jnp.where(b < 0, -m, m)


def kernel(
    r_hbm, s_hbm, c_hbm, g_ref, res_ref,
    r_ref, sall, cpad, cmd_t, acc, csend, crecv, near_s, near_r, far_s, far_r, sum_s, sum_r,
    ring_s, ring_r, xsend, xrecv, rall, turned,
    in_sem, s_ss, s_rs, ss, rs,
):
    row, col = lax.axis_index("row"), lax.axis_index("col")
    y, xh = row // 2, row % 2
    z, xl, core = col // 4, (col // 2) % 2, col % 2
    quad = xl * 2 + core
    y_up = (((y + 1) % 4) * 2 + xh, col)
    y_dn = (((y + 3) % 4) * 2 + xh, col)
    x_far = (y * 2 + 1 - xh, col)
    z_up = (row, ((z + 1) % 8) * 4 + quad)
    z_dn = (row, ((z + 7) % 8) * 4 + quad)
    z_up2 = (row, ((z + 2) % 8) * 4 + quad)
    z_dn2 = (row, ((z + 6) % 8) * 4 + quad)
    x_near = (row, z * 4 + (1 - xl) * 2 + core)
    twin = (row, z * 4 + xl * 2 + 1 - core)

    barrier = pltpu.get_barrier_semaphore()
    for device in (y_up, y_dn, x_far, z_up, z_dn, z_up2, z_dn2, x_near, twin):
        pl.semaphore_signal(barrier, inc=1, device_id=device, device_id_type=MESH)

    s_in = pltpu.make_async_copy(s_hbm, sall.at[0], in_sem.at[0])
    r_in = pltpu.make_async_copy(r_hbm, r_ref, in_sem.at[1])
    s_in.start()
    r_in.start()
    cpad[...] = jnp.zeros_like(cpad)
    def remote(src, dst, send, recv, device):
        return pltpu.make_async_remote_copy(
            src_ref=src, dst_ref=dst, send_sem=send, recv_sem=recv,
            device_id=device, device_id_type=MESH,
        )

    mid = DEPTH // 2
    lo, hi, every = pl.ds(0, mid), pl.ds(mid, mid), pl.ds(0, DEPTH)
    most, rest = pl.ds(0, 3 * DEPTH // 4), pl.ds(3 * DEPTH // 4, DEPTH // 4)
    left, right = pl.ds(0, 128), pl.ds(128, 128)
    s_moves = [
        remote(
            s_hbm.at[r0, c0] if i == 0 else sall.at[i, r0, c0],
            sall.at[j, r0, c1], s_ss.at[n], s_rs.at[n], device,
        )
        for n, (i, j, r0, c0, c1, device) in enumerate((
            (0, 1, every, left, left, y_up),
            (0, 1, every, left, right, y_dn),
            (0, 2, every, right, left, y_up),
            (0, 2, every, right, right, y_dn),
            (0, 3, every, left, left, x_far),
            (0, 3, every, right, right, x_far),
            (1, 4, lo, left, left, y_up),
            (1, 4, hi, right, left, y_dn),
            (2, 4, lo, left, right, y_up),
            (2, 4, hi, right, right, y_dn),
            (3, 5, every, left, left, y_up),
            (3, 5, every, left, right, y_dn),
            (3, 6, most, right, left, y_up),
            (3, 6, most, right, right, y_dn),
            (4, 7, every, left, left, x_far),
            (4, 7, every, right, right, x_far),
            (2, 6, rest, left, left, x_far),
            (2, 6, rest, right, right, x_far),
        ))
    ]
    passes = [
        ((0, 1), (6, 7)), ((2, 3), (8, 9, 16, 17)), ((4,), (10, 11)), ((5,), (12, 13)), ((6, 7), (14,)),
        ((8, 9), (15,)),
    ]
    dy = (z // 2 + 4 - y) % 4
    dx = (z % 2 + 2 - xh) % 2
    beside = (dy == 1) | (dy == 3)
    my_slot = jnp.where(beside, 1 + 4 * dx + xl, jnp.where(dy == 0, 3 * dx, 4 + 3 * dx))
    my_half = jnp.where(beside, (dy == 1).astype(jnp.int32), xl)
    c_in = pltpu.make_async_copy(
        c_hbm,
        cpad.at[pl.ds(pl.multiple_of(my_half * 128 + core * 64, 64), 64)],
        in_sem.at[2],
    )
    c_in.start()
    pl.semaphore_wait(barrier, 9)
    for i in (0, 1, 4, 2, 3, 5):
        s_moves[i].start()
    s_in.wait()

    c_in.wait()
    cmd_t[...] = cpad[...].T
    g_ref[...] = jnp.zeros_like(g_ref)
    r_in.wait()

    own0 = core * HALF
    other0 = (1 - core) * HALF

    def rows(start, size):
        return pl.ds(pl.multiple_of(start, size), size)

    def core_move(g):
        return remote(csend.at[g], crecv.at[g], ss.at[g, 0], rs.at[g, 0], twin)

    one, two = (z_up, z_dn), (z_up2, z_dn2)

    def out_core(g):
        here = rall.at[g, rows(own0, HALF)]
        return remote(here, here, ss.at[g, 16], rs.at[g, 16], twin)

    def in_core(g):
        here = rall.at[g, rows(other0, HALF)]
        return remote(here, here, ss.at[g, 16], rs.at[g, 16], twin)

    def pass_on(n):
        arrived, onward = passes[n]
        for i in arrived:
            s_moves[i].wait_recv()
        for i in onward:
            s_moves[i].start()

    def stage_predict(g):
        if g >= 5:
            s_moves[2 * g].wait_recv()
            s_moves[2 * g + 1].wait_recv()
        if g == 6:
            s_moves[16].wait_recv()
            s_moves[17].wait_recv()

        mine = (g == my_slot).astype(jnp.float32)
        tile = 512

        def predicted(start):
            p = jnp.dot(
                r_ref[rows(start, tile), :], sall[g], preferred_element_type=jnp.float32
            )
            return p - cmd_t[rows(start, tile), :] * mine

        @pl.loop(0, HALF // tile)
        def _(i):
            csend[g, rows(i * tile, tile), :] = code(predicted(other0 + i * tile))

        core_move(g).start()

        @pl.loop(0, HALF // tile)
        def _(i):
            acc[g, rows(i * tile, tile), :] = predicted(own0 + i * tile)

    scale_factor = 1.0 / jnp.sqrt(jnp.float32(2048))

    def add_gradient(g, start, last):
        here = rows(start, HALF)
        added = g_ref[here, :] + lax.dot_general(
            rall[g, here, :], sall[g], (((1,), (1,)), ((), ())),
            preferred_element_type=jnp.float32,
        )
        g_ref[here, :] = added * scale_factor if g == last else added

    def share(g):
        out_core(g).start()
        add_gradient(g, own0, LAST_OWN)

    def with_twin(g, here):
        return acc[g, here, :] + decode(crecv[g, here, :])

    def tree(size, base, term):
        half = size // 2
        first, second = pl.ds(0, size), pl.ds(size, size)

        def part(at, count=size, skip=0):
            return rows(base + ((z + at + 8) % 8) * size + skip, count)

        def near_move(g, d):
            here = near_s.at[g, d, pl.ds(0, 2 * size)]
            there = near_r.at[g, d, pl.ds(0, 2 * size)]
            return remote(here, there, ss.at[g, 1 + d], rs.at[g, 1 + d], one[d])

        def far_move(g, d):
            here, there = far_s.at[g, d, pl.ds(0, half)], far_r.at[g, d, pl.ds(0, half)]
            return remote(here, there, ss.at[g, 3 + d], rs.at[g, 3 + d], two[d])

        def sum_move(g, d):
            here, there = sum_s.at[g, d, first], sum_r.at[g, d, first]
            return remote(here, there, ss.at[g, 5 + d], rs.at[g, 5 + d], two[d])

        def spread(g, d, n, at, device, count=size, skip=0):
            start = own0 + base + ((z + at + 8) % 8) * size + skip
            here = rall.at[g, rows(start, count)]
            return remote(here, here, ss.at[g, n + d], rs.at[g, n + d], device)

        def out_1(g, d):
            return spread(g, d, 8, 0, one[d])

        def in_1(g, d):
            return spread(g, d, 8, (-1, 1)[d], one[d])

        def out_2(g, d):
            return spread(g, d, 10, 0, two[d])

        def in_2(g, d):
            return spread(g, d, 10, (-2, 2)[d], two[d])

        def out_3(g, d):
            return spread(g, d, 12, (-2, 2)[d], one[d])

        def in_3(g, d):
            return spread(g, d, 12, (-3, 3)[d], one[d])

        def out_4(g, d):
            return spread(g, d, 14, (-2, 2)[d], two[d], half, d * half)

        def in_4(g, d):
            return spread(g, d, 14, 4, two[d], half, d * half)

        def send_terms(g):
            for d, sign in ((0, 1), (1, -1)):
                far_s[g, d, pl.ds(0, half), :] = code(term(g, part(4, half, d * half)))
                far_move(g, d).start()
                near_s[g, d, second, :] = code(term(g, part(3 * sign)))
                near_s[g, d, first, :] = code(term(g, part(sign)))
                near_move(g, d).start()

        def send_sums(g):
            for d, sign in ((0, 1), (1, -1)):
                near_move(g, d).wait_recv()
                far_move(g, d).wait_recv()
                for h in (0, 1):
                    total = term(g, part(2 * sign, half, h * half)) + decode(
                        near_r[g, d, pl.ds(size + h * half, half), :]
                    )
                    if h == d:
                        total = total + decode(far_r[g, d, pl.ds(0, half), :])
                    sum_s[g, d, pl.ds(h * half, half), :] = code(total)
                sum_move(g, d).start()

        def total(g):
            total = term(g, part(0))
            for d in (0, 1):
                sum_move(g, d).wait_recv()
                total = total + decode(near_r[g, d, first, :]) + decode(sum_r[g, d, first, :])
            return total

        def hand_round(g, residual):
            rall[g, rows(own0 + base + z * size, size), :] = residual.astype(jnp.bfloat16)
            for d in (0, 1):
                out_2(g, d).start()
            for d in (0, 1):
                out_1(g, d).start()

        def hand_on(g):
            for d in (0, 1):
                in_2(g, d).wait_recv()
                out_4(g, d).start()
                out_3(g, d).start()

        def all_here(g):
            for d in (0, 1):
                in_1(g, d).wait_recv()
                in_3(g, d).wait_recv()
                in_4(g, d).wait_recv()

        def sent(g):
            for move in (near_move, far_move, sum_move, out_1, out_2, out_3, out_4):
                for d in (0, 1):
                    move(g, d).wait_send()

        return part, send_terms, send_sums, total, hand_round, hand_on, all_here, sent

    def x_move(g):
        here, there = xsend.at[g, pl.ds(0, SLICE)], xrecv.at[g, pl.ds(0, SLICE)]
        return remote(here, there, ss.at[g, 18], rs.at[g, 18], x_near)

    (
        two_part, two_terms, two_sums, two_total, two_round, two_on, two_here, two_sent,
    ) = tree(SLICE, 0, with_twin)

    def two_1(g):
        core_move(g).wait_recv()
        two_terms(g)

    def two_3(g):
        total = two_total(g)
        acc[g, two_part(0), :] = total
        xsend[g, pl.ds(0, SLICE), :] = code(total)
        x_move(g).start()

    def two_4(g):
        x_move(g).wait_recv()
        two_round(g, acc[g, two_part(0), :] + decode(xrecv[g, pl.ds(0, SLICE), :]))

    def two_6(g):
        two_here(g)
        share(g)

    quarter = HALF // 2

    def half_move(g):
        return remote(xsend.at[g], xrecv.at[g], ss.at[g, 7], rs.at[g, 7], x_near)

    def out_x(g):
        here = rall.at[g, rows(own0 + xl * quarter, quarter)]
        return remote(here, here, ss.at[g, 17], rs.at[g, 17], x_near)

    def in_x(g):
        here = rall.at[g, rows(own0 + (1 - xl) * quarter, quarter)]
        return remote(here, here, ss.at[g, 17], rs.at[g, 17], x_near)

    xf_part, xf_terms, xf_sums, xf_total, xf_round, xf_on, xf_here, xf_sent = tree(
        SLICE // 2, xl * quarter, lambda g, here: acc[g, here, :]
    )

    def xf_1(g):
        core_move(g).wait_recv()

        @pl.loop(0, quarter // SLICE)
        def _(i):
            here = rows((1 - xl) * quarter + i * SLICE, SLICE)
            xsend[g, rows(i * SLICE, SLICE), :] = code(with_twin(g, here))

        half_move(g).start()

    def xf_2(g):
        half_move(g).wait_recv()

        @pl.loop(0, quarter // SLICE)
        def _(i):
            here = rows(xl * quarter + i * SLICE, SLICE)
            other = decode(xrecv[g, rows(i * SLICE, SLICE), :])
            acc[g, here, :] = with_twin(g, here) + other

        xf_terms(g)

    def xf_4(g):
        xf_round(g, xf_total(g))

    def xf_6(g):
        xf_here(g)
        out_x(g).start()

    def xf_7(g):
        in_x(g).wait_recv()
        share(g)

    def ring_part(at):
        return rows(((z + at + 8) % 8) * SLICE, SLICE)

    def ring_here(g, at):
        return rall.at[g, rows(own0 + ((z + at + 8) % 8) * SLICE, SLICE)]

    def up_move(g, i):
        return remote(ring_s.at[g, i], ring_r.at[g, i], ss.at[g, 1 + i], rs.at[g, 1 + i], z_up)

    def dn_move(g, i):
        return remote(
            ring_s.at[g, 4 + i], ring_r.at[g, 4 + i], ss.at[g, 5 + i], rs.at[g, 5 + i], z_dn
        )

    def out_up(g, i):
        here = ring_here(g, -i)
        return remote(here, here, ss.at[g, 9 + i], rs.at[g, 9 + i], z_up)

    def in_up(g, i):
        here = ring_here(g, -i - 1)
        return remote(here, here, ss.at[g, 9 + i], rs.at[g, 9 + i], z_up)

    def out_dn(g, i):
        here = ring_here(g, i)
        return remote(here, here, ss.at[g, 12 + i], rs.at[g, 12 + i], z_dn)

    def in_dn(g, i):
        here = ring_here(g, i + 1)
        return remote(here, here, ss.at[g, 12 + i], rs.at[g, 12 + i], z_dn)

    def send_up(g, i):
        total = with_twin(g, ring_part(4 - i))
        if i:
            up_move(g, i - 1).wait_recv()
            total = total + decode(ring_r[g, i - 1])
        ring_s[g, i] = code(total)
        up_move(g, i).start()

    def send_dn(g, i):
        total = with_twin(g, ring_part(i - 3))
        if i:
            dn_move(g, i - 1).wait_recv()
            total = total + decode(ring_r[g, 3 + i])
        ring_s[g, 4 + i] = code(total)
        dn_move(g, i).start()

    def ring_1(g):
        core_move(g).wait_recv()
        send_up(g, 0)

    def ring_2(g, i=1):
        send_dn(g, i - 1)
        send_up(g, i)

    def ring_5(g):
        dn_move(g, 2).wait_recv()
        up_move(g, 3).wait_recv()
        total = with_twin(g, ring_part(0)) + decode(ring_r[g, 6]) + decode(ring_r[g, 3])
        acc[g, ring_part(0), :] = total
        xsend[g, pl.ds(0, SLICE), :] = code(total)
        x_move(g).start()

    def ring_6(g):
        x_move(g).wait_recv()
        low = acc[g, ring_part(0), :] + decode(xrecv[g, pl.ds(0, SLICE), :])
        rall[g, rows(own0 + z * SLICE, SLICE), :] = low.astype(jnp.bfloat16)
        out_dn(g, 0).start()
        out_up(g, 0).start()

    def ring_7(g, i=0):
        in_dn(g, i).wait_recv()
        out_dn(g, i + 1).start()
        in_up(g, i).wait_recv()
        out_up(g, i + 1).start()

    def ring_9(g):
        in_dn(g, 2).wait_recv()
        out_dn(g, 3).start()
        in_up(g, 2).wait_recv()

    def ring_10(g):
        in_dn(g, 3).wait_recv()
        share(g)

    def ring_sent(g):
        for i in range(4):
            up_move(g, i).wait_send()
            out_dn(g, i).wait_send()
        for i in range(3):
            dn_move(g, i).wait_send()
            out_up(g, i).wait_send()

    def stage_gradient(g):
        in_core(g).wait_recv()
        add_gradient(g, other0, LAST_OTHER)

        @pl.when(g == my_slot)
        def _():
            half = rall[g, :, pl.ds(pl.multiple_of(my_half * 128, 128), 128)]
            turned[...] = half.astype(jnp.float32).T
            res_ref[...] = turned[rows(core * 64, 64), :]

        core_move(g).wait_send()
        out_core(g).wait_send()

        if g in KINDS["two"]:
            two_sent(g)
            x_move(g).wait_send()

        if g in KINDS["xf"]:
            xf_sent(g)
            half_move(g).wait_send()
            out_x(g).wait_send()

        if g in KINDS["ring"]:
            ring_sent(g)
            x_move(g).wait_send()

    stages = {
        "pass_on": pass_on, "predict": stage_predict, "gradient": stage_gradient,
        "two_1": two_1, "two_2": two_sums, "two_3": two_3, "two_4": two_4, "two_5": two_on,
        "two_6": two_6,
        "xf_1": xf_1, "xf_2": xf_2, "xf_3": xf_sums, "xf_4": xf_4, "xf_5": xf_on, "xf_6": xf_6,
        "xf_7": xf_7,
        "ring_1": ring_1, "ring_2": ring_2, "ring_3": functools.partial(ring_2, i=2),
        "ring_4": functools.partial(ring_2, i=3), "ring_5": ring_5, "ring_6": ring_6,
        "ring_7": ring_7, "ring_8": functools.partial(ring_7, i=1), "ring_9": ring_9,
        "ring_10": ring_10,
    }

    for name, g in ORDER:
        stages[name](g)

    for move in s_moves:
        move.wait_send()


def finish(g_ref, res_ref, g_hbm, res_hbm, sem):
    size = FULL // PIECES
    moves = [pltpu.make_async_copy(res_ref, res_hbm, sem.at[PIECES])]
    for i in range(PIECES):
        here = pl.ds(i * size, size)
        moves.append(pltpu.make_async_copy(g_ref.at[here], g_hbm.at[here], sem.at[i]))
    for move in moves:
        move.start()
    for move in moves:
        move.wait()


def on_device(reconstructor, slopes, commands):
    vmem = pltpu.VMEM
    gradient, residual = pl.pallas_call(
        kernel,
        out_shape=(
            pltpu.VMEM((FULL, DEPTH), jnp.float32),
            pltpu.VMEM((64, FULL), jnp.float32),
        ),
        in_specs=[pl.BlockSpec(memory_space=pl.ANY)] * 3,
        out_specs=[pl.BlockSpec(memory_space=pltpu.VMEM)] * 2,
        scratch_shapes=[
            vmem((FULL, DEPTH), jnp.bfloat16),
            vmem((BLOCKS, DEPTH, BLOCK), jnp.bfloat16),
            vmem((BLOCK, FULL), jnp.float32),
            vmem((FULL, BLOCK), jnp.float32),
            vmem((BLOCKS, HALF, BLOCK), jnp.float32),
            vmem((BLOCKS, HALF, BLOCK), jnp.bfloat16),
            vmem((BLOCKS, HALF, BLOCK), jnp.bfloat16),
            vmem((BLOCKS, 2, 2 * SLICE, BLOCK), jnp.bfloat16),
            vmem((BLOCKS, 2, 2 * SLICE, BLOCK), jnp.bfloat16),
            vmem((BLOCKS, 2, SLICE // 2, BLOCK), jnp.bfloat16),
            vmem((BLOCKS, 2, SLICE // 2, BLOCK), jnp.bfloat16),
            vmem((BLOCKS, 2, SLICE, BLOCK), jnp.bfloat16),
            vmem((BLOCKS, 2, SLICE, BLOCK), jnp.bfloat16),
            vmem((BLOCKS, 7, SLICE, BLOCK), jnp.bfloat16),
            vmem((BLOCKS, 7, SLICE, BLOCK), jnp.bfloat16),
            vmem((BLOCKS, HALF // 2, BLOCK), jnp.bfloat16),
            vmem((BLOCKS, HALF // 2, BLOCK), jnp.bfloat16),
            vmem((BLOCKS, FULL, BLOCK), jnp.bfloat16),
            vmem((128, FULL), jnp.float32),
            pltpu.SemaphoreType.DMA((3,)),
            pltpu.SemaphoreType.DMA((18,)),
            pltpu.SemaphoreType.DMA((18,)),
            pltpu.SemaphoreType.DMA((BLOCKS, 19)),
            pltpu.SemaphoreType.DMA((BLOCKS, 19)),
        ],
        compiler_params=pltpu.CompilerParams(
            collective_id=0, has_side_effects=True, vmem_limit_bytes=56 << 20
        ),
        cost_estimate=pl.CostEstimate(
            flops=4 * 2048 * FULL * DEPTH, bytes_accessed=9 << 20, transcendentals=0
        ),
    )(reconstructor, slopes, commands)
    return pl.pallas_call(
        finish,
        out_shape=(
            jax.ShapeDtypeStruct((FULL, DEPTH), jnp.float32),
            jax.ShapeDtypeStruct((64, FULL), jnp.float32),
        ),
        in_specs=[pl.BlockSpec(memory_space=pltpu.VMEM)] * 2,
        out_specs=[pl.BlockSpec(memory_space=pl.ANY)] * 2,
        scratch_shapes=[
            pltpu.SemaphoreType.DMA((PIECES + 1,)),
        ],
        compiler_params=pltpu.CompilerParams(vmem_limit_bytes=4 << 20),
    )(gradient, residual)


def solution(mesh):
    in_specs = (P("row", "col"), P("col", "row"), P("col", "row"))
    out_specs = (P("row", "col"), P("col", "row"))
    return jax.shard_map(
        on_device, mesh=mesh, in_specs=in_specs, out_specs=out_specs, check_vma=False
    )
```

```python
import functools

import jax
import jax.numpy as jnp
from jax import lax
from jax.experimental import pallas as pl
from jax.experimental.pallas import tpu as pltpu
from jax.sharding import PartitionSpec as P

MESH = pl.DeviceIdType.MESH

FULL = 1024
HALF = 512
SLICE = 64
DEPTH = 1280
BLOCK = 256
BLOCKS = 8
PIECES = 8
KINDS = {
    "two": (0, 7,),
    "xf": (1, 6,),
    "ring": (2, 3, 4, 5,),
}
ORDER = (
    ("predict", 0), ("two_1", 0), ("pass_on", 0), ("two_2", 0), ("predict", 1), ("xf_1", 1),
    ("pass_on", 1), ("pass_on", 2), ("pass_on", 3), ("predict", 2), ("two_3", 0), ("ring_1", 2),
    ("xf_2", 1), ("predict", 3), ("pass_on", 4), ("ring_2", 2), ("ring_1", 3), ("pass_on", 5),
    ("predict", 4), ("xf_3", 1), ("ring_1", 4), ("ring_3", 2), ("two_4", 0), ("ring_2", 3),
    ("ring_2", 4), ("ring_4", 2), ("xf_4", 1), ("predict", 5), ("ring_1", 5), ("ring_3", 3),
    ("ring_3", 4), ("two_5", 0), ("ring_5", 2), ("xf_5", 1), ("predict", 6), ("ring_2", 5),
    ("ring_4", 3), ("xf_1", 6), ("ring_4", 4), ("ring_6", 2), ("predict", 7), ("ring_3", 5),
    ("ring_5", 3), ("two_1", 7), ("ring_5", 4), ("xf_2", 6), ("ring_4", 5), ("xf_6", 1),
    ("ring_6", 4), ("ring_7", 2), ("ring_6", 3), ("xf_3", 6), ("ring_5", 5), ("two_2", 7),
    ("ring_7", 4), ("two_6", 0), ("ring_8", 2), ("xf_7", 1), ("ring_7", 3), ("xf_4", 6),
    ("ring_6", 5), ("gradient", 0), ("ring_8", 4), ("two_3", 7), ("ring_9", 2), ("ring_8", 3),
    ("xf_5", 6), ("gradient", 1), ("ring_7", 5), ("ring_9", 4), ("two_4", 7), ("ring_10", 2),
    ("xf_6", 6), ("ring_8", 5), ("gradient", 2), ("ring_9", 3), ("two_5", 7), ("ring_10", 4),
    ("ring_9", 5), ("gradient", 4), ("ring_10", 3), ("xf_7", 6), ("gradient", 3), ("two_6", 7),
    ("ring_10", 5), ("gradient", 6), ("gradient", 7), ("gradient", 5),
)
OWN_ENDS, OTHER_ENDS = (0, 5), (0, 5)


def code(v):
    return (v * jnp.abs(v) * (v * v)).astype(jnp.bfloat16)


def decode(b):
    b = b.astype(jnp.float32)
    m = jnp.abs(b)
    m = m * lax.rsqrt(jnp.maximum(m, 1e-36))
    m = m * lax.rsqrt(jnp.maximum(m, 1e-18))
    return jnp.where(b < 0, -m, m)


def kernel(
    r_hbm, s_hbm, c_hbm, g_ref, res_ref,
    r_ref, sall, cpad, cmd_t, acc, csend, crecv, near_s, near_r, far_s, far_r, sum_s, sum_r,
    ring_s, ring_r, xsend, xrecv, rall, turned,
    in_sem, s_ss, s_rs, ss, rs,
):
    row, col = lax.axis_index("row"), lax.axis_index("col")
    y, xh = row // 2, row % 2
    z, xl, core = col // 4, (col // 2) % 2, col % 2
    quad = xl * 2 + core
    y_up = (((y + 1) % 4) * 2 + xh, col)
    y_dn = (((y + 3) % 4) * 2 + xh, col)
    x_far = (y * 2 + 1 - xh, col)
    z_up = (row, ((z + 1) % 8) * 4 + quad)
    z_dn = (row, ((z + 7) % 8) * 4 + quad)
    z_up2 = (row, ((z + 2) % 8) * 4 + quad)
    z_dn2 = (row, ((z + 6) % 8) * 4 + quad)
    x_near = (row, z * 4 + (1 - xl) * 2 + core)
    twin = (row, z * 4 + xl * 2 + 1 - core)

    barrier = pltpu.get_barrier_semaphore()
    for device in (y_up, y_dn, x_far, z_up, z_dn, z_up2, z_dn2, x_near, twin):
        pl.semaphore_signal(barrier, inc=1, device_id=device, device_id_type=MESH)

    s_in = pltpu.make_async_copy(s_hbm, sall.at[0], in_sem.at[0])
    r_in = pltpu.make_async_copy(r_hbm, r_ref, in_sem.at[1])
    s_in.start()
    r_in.start()
    cpad[...] = jnp.zeros_like(cpad)
    def remote(src, dst, send, recv, device):
        return pltpu.make_async_remote_copy(
            src_ref=src, dst_ref=dst, send_sem=send, recv_sem=recv,
            device_id=device, device_id_type=MESH,
        )

    mid = DEPTH // 2
    lo, hi, every = pl.ds(0, mid), pl.ds(mid, mid), pl.ds(0, DEPTH)
    most, rest = pl.ds(0, 3 * DEPTH // 4), pl.ds(3 * DEPTH // 4, DEPTH // 4)
    left, right = pl.ds(0, 128), pl.ds(128, 128)
    s_moves = [
        remote(
            s_hbm.at[r0, c0] if i == 0 else sall.at[i, r0, c0],
            sall.at[j, r0, c1], s_ss.at[n], s_rs.at[n], device,
        )
        for n, (i, j, r0, c0, c1, device) in enumerate((
            (0, 1, every, left, left, y_up),
            (0, 1, every, left, right, y_dn),
            (0, 2, every, right, left, y_up),
            (0, 2, every, right, right, y_dn),
            (0, 3, every, left, left, x_far),
            (0, 3, every, right, right, x_far),
            (1, 4, lo, left, left, y_up),
            (1, 4, hi, right, left, y_dn),
            (2, 4, lo, left, right, y_up),
            (2, 4, hi, right, right, y_dn),
            (3, 5, every, left, left, y_up),
            (3, 5, every, left, right, y_dn),
            (3, 6, most, right, left, y_up),
            (3, 6, most, right, right, y_dn),
            (4, 7, every, left, left, x_far),
            (4, 7, every, right, right, x_far),
            (2, 6, rest, left, left, x_far),
            (2, 6, rest, right, right, x_far),
        ))
    ]
    passes = [
        ((0, 1), (6, 7)), ((2, 3), (8, 9, 16, 17)), ((4,), (10, 11)), ((5,), (12, 13)), ((6, 7), (14,)),
        ((8, 9), (15,)),
    ]
    dy = (z // 2 + 4 - y) % 4
    dx = (z % 2 + 2 - xh) % 2
    beside = (dy == 1) | (dy == 3)
    my_slot = jnp.where(beside, 1 + 4 * dx + xl, jnp.where(dy == 0, 3 * dx, 4 + 3 * dx))
    my_half = jnp.where(beside, (dy == 1).astype(jnp.int32), xl)
    c_in = pltpu.make_async_copy(
        c_hbm,
        cpad.at[pl.ds(pl.multiple_of(my_half * 128 + core * 64, 64), 64)],
        in_sem.at[2],
    )
    c_in.start()
    pl.semaphore_wait(barrier, 9)
    for i in (0, 1, 4, 2, 3, 5):
        s_moves[i].start()
    s_in.wait()

    c_in.wait()
    cmd_t[...] = cpad[...].T
    r_in.wait()

    own0 = core * HALF
    other0 = (1 - core) * HALF

    def rows(start, size):
        return pl.ds(pl.multiple_of(start, size), size)

    def core_move(g):
        return remote(csend.at[g], crecv.at[g], ss.at[g, 0], rs.at[g, 0], twin)

    one, two = (z_up, z_dn), (z_up2, z_dn2)

    def out_core(g):
        here = rall.at[g, rows(own0, HALF)]
        return remote(here, here, ss.at[g, 16], rs.at[g, 16], twin)

    def in_core(g):
        here = rall.at[g, rows(other0, HALF)]
        return remote(here, here, ss.at[g, 16], rs.at[g, 16], twin)

    def pass_on(n):
        arrived, onward = passes[n]
        for i in arrived:
            s_moves[i].wait_recv()
        for i in onward:
            s_moves[i].start()

    def stage_predict(g):
        if g >= 5:
            s_moves[2 * g].wait_recv()
            s_moves[2 * g + 1].wait_recv()
        if g == 6:
            s_moves[16].wait_recv()
            s_moves[17].wait_recv()

        mine = (g == my_slot).astype(jnp.float32)
        tile = 512

        def predicted(start):
            p = jnp.dot(
                r_ref[rows(start, tile), :], sall[g], preferred_element_type=jnp.float32
            )
            return p - cmd_t[rows(start, tile), :] * mine

        @pl.loop(0, HALF // tile)
        def _(i):
            csend[g, rows(i * tile, tile), :] = code(predicted(other0 + i * tile))

        core_move(g).start()

        @pl.loop(0, HALF // tile)
        def _(i):
            acc[g, rows(i * tile, tile), :] = predicted(own0 + i * tile)

    scale_factor = 1.0 / jnp.sqrt(jnp.float32(2048))

    def add_gradient(g, start, ends):
        here = rows(start, HALF)
        added = lax.dot_general(
            rall[g, here, :], sall[g], (((1,), (1,)), ((), ())),
            preferred_element_type=jnp.float32,
        )
        if g != ends[0]:
            added = g_ref[here, :] + added
        g_ref[here, :] = added * scale_factor if g == ends[1] else added

    def share(g):
        out_core(g).start()
        add_gradient(g, own0, OWN_ENDS)

    def with_twin(g, here):
        return acc[g, here, :] + decode(crecv[g, here, :])

    def tree(size, base, term):
        half = size // 2
        first, second = pl.ds(0, size), pl.ds(size, size)

        def part(at, count=size, skip=0):
            return rows(base + ((z + at + 8) % 8) * size + skip, count)

        def near_move(g, d):
            here = near_s.at[g, d, pl.ds(0, 2 * size)]
            there = near_r.at[g, d, pl.ds(0, 2 * size)]
            return remote(here, there, ss.at[g, 1 + d], rs.at[g, 1 + d], one[d])

        def far_move(g, d):
            here, there = far_s.at[g, d, pl.ds(0, half)], far_r.at[g, d, pl.ds(0, half)]
            return remote(here, there, ss.at[g, 3 + d], rs.at[g, 3 + d], two[d])

        def sum_move(g, d):
            here, there = sum_s.at[g, d, first], sum_r.at[g, d, first]
            return remote(here, there, ss.at[g, 5 + d], rs.at[g, 5 + d], two[d])

        def spread(g, d, n, at, device, count=size, skip=0):
            start = own0 + base + ((z + at + 8) % 8) * size + skip
            here = rall.at[g, rows(start, count)]
            return remote(here, here, ss.at[g, n + d], rs.at[g, n + d], device)

        def out_1(g, d):
            return spread(g, d, 8, 0, one[d])

        def in_1(g, d):
            return spread(g, d, 8, (-1, 1)[d], one[d])

        def out_2(g, d):
            return spread(g, d, 10, 0, two[d])

        def in_2(g, d):
            return spread(g, d, 10, (-2, 2)[d], two[d])

        def out_3(g, d):
            return spread(g, d, 12, (-2, 2)[d], one[d])

        def in_3(g, d):
            return spread(g, d, 12, (-3, 3)[d], one[d])

        def out_4(g, d):
            return spread(g, d, 14, (-2, 2)[d], two[d], half, d * half)

        def in_4(g, d):
            return spread(g, d, 14, 4, two[d], half, d * half)

        def send_terms(g):
            for d, sign in ((0, 1), (1, -1)):
                far_s[g, d, pl.ds(0, half), :] = code(term(g, part(4, half, d * half)))
                far_move(g, d).start()
                near_s[g, d, second, :] = code(term(g, part(3 * sign)))
                near_s[g, d, first, :] = code(term(g, part(sign)))
                near_move(g, d).start()

        def send_sums(g):
            for d, sign in ((0, 1), (1, -1)):
                near_move(g, d).wait_recv()
                far_move(g, d).wait_recv()
                for h in (0, 1):
                    total = term(g, part(2 * sign, half, h * half)) + decode(
                        near_r[g, d, pl.ds(size + h * half, half), :]
                    )
                    if h == d:
                        total = total + decode(far_r[g, d, pl.ds(0, half), :])
                    sum_s[g, d, pl.ds(h * half, half), :] = code(total)
                sum_move(g, d).start()

        def total(g):
            total = term(g, part(0))
            for d in (0, 1):
                sum_move(g, d).wait_recv()
                total = total + decode(near_r[g, d, first, :]) + decode(sum_r[g, d, first, :])
            return total

        def hand_round(g, residual):
            rall[g, rows(own0 + base + z * size, size), :] = residual.astype(jnp.bfloat16)
            for d in (0, 1):
                out_2(g, d).start()
            for d in (0, 1):
                out_1(g, d).start()

        def hand_on(g):
            for d in (0, 1):
                in_2(g, d).wait_recv()
                out_4(g, d).start()
                out_3(g, d).start()

        def all_here(g):
            for d in (0, 1):
                in_1(g, d).wait_recv()
                in_3(g, d).wait_recv()
                in_4(g, d).wait_recv()

        def sent(g):
            for move in (near_move, far_move, sum_move, out_1, out_2, out_3, out_4):
                for d in (0, 1):
                    move(g, d).wait_send()

        return part, send_terms, send_sums, total, hand_round, hand_on, all_here, sent

    def x_move(g):
        here, there = xsend.at[g, pl.ds(0, SLICE)], xrecv.at[g, pl.ds(0, SLICE)]
        return remote(here, there, ss.at[g, 18], rs.at[g, 18], x_near)

    (
        two_part, two_terms, two_sums, two_total, two_round, two_on, two_here, two_sent,
    ) = tree(SLICE, 0, with_twin)

    def two_1(g):
        core_move(g).wait_recv()
        two_terms(g)

    def two_3(g):
        total = two_total(g)
        acc[g, two_part(0), :] = total
        xsend[g, pl.ds(0, SLICE), :] = code(total)
        x_move(g).start()

    def two_4(g):
        x_move(g).wait_recv()
        two_round(g, acc[g, two_part(0), :] + decode(xrecv[g, pl.ds(0, SLICE), :]))

    def two_6(g):
        two_here(g)
        share(g)

    quarter = HALF // 2

    def half_move(g):
        return remote(xsend.at[g], xrecv.at[g], ss.at[g, 7], rs.at[g, 7], x_near)

    def out_x(g):
        here = rall.at[g, rows(own0 + xl * quarter, quarter)]
        return remote(here, here, ss.at[g, 17], rs.at[g, 17], x_near)

    def in_x(g):
        here = rall.at[g, rows(own0 + (1 - xl) * quarter, quarter)]
        return remote(here, here, ss.at[g, 17], rs.at[g, 17], x_near)

    xf_part, xf_terms, xf_sums, xf_total, xf_round, xf_on, xf_here, xf_sent = tree(
        SLICE // 2, xl * quarter, lambda g, here: acc[g, here, :]
    )

    def xf_1(g):
        core_move(g).wait_recv()

        @pl.loop(0, quarter // SLICE)
        def _(i):
            here = rows((1 - xl) * quarter + i * SLICE, SLICE)
            xsend[g, rows(i * SLICE, SLICE), :] = code(with_twin(g, here))

        half_move(g).start()

    def xf_2(g):
        half_move(g).wait_recv()

        @pl.loop(0, quarter // SLICE)
        def _(i):
            here = rows(xl * quarter + i * SLICE, SLICE)
            other = decode(xrecv[g, rows(i * SLICE, SLICE), :])
            acc[g, here, :] = with_twin(g, here) + other

        xf_terms(g)

    def xf_4(g):
        xf_round(g, xf_total(g))

    def xf_6(g):
        xf_here(g)
        out_x(g).start()

    def xf_7(g):
        in_x(g).wait_recv()
        share(g)

    def ring_part(at):
        return rows(((z + at + 8) % 8) * SLICE, SLICE)

    def ring_here(g, at):
        return rall.at[g, rows(own0 + ((z + at + 8) % 8) * SLICE, SLICE)]

    def up_move(g, i):
        return remote(ring_s.at[g, i], ring_r.at[g, i], ss.at[g, 1 + i], rs.at[g, 1 + i], z_up)

    def dn_move(g, i):
        return remote(
            ring_s.at[g, 4 + i], ring_r.at[g, 4 + i], ss.at[g, 5 + i], rs.at[g, 5 + i], z_dn
        )

    def out_up(g, i):
        here = ring_here(g, -i)
        return remote(here, here, ss.at[g, 9 + i], rs.at[g, 9 + i], z_up)

    def in_up(g, i):
        here = ring_here(g, -i - 1)
        return remote(here, here, ss.at[g, 9 + i], rs.at[g, 9 + i], z_up)

    def out_dn(g, i):
        here = ring_here(g, i)
        return remote(here, here, ss.at[g, 12 + i], rs.at[g, 12 + i], z_dn)

    def in_dn(g, i):
        here = ring_here(g, i + 1)
        return remote(here, here, ss.at[g, 12 + i], rs.at[g, 12 + i], z_dn)

    def send_up(g, i):
        total = with_twin(g, ring_part(4 - i))
        if i:
            up_move(g, i - 1).wait_recv()
            total = total + decode(ring_r[g, i - 1])
        ring_s[g, i] = code(total)
        up_move(g, i).start()

    def send_dn(g, i):
        total = with_twin(g, ring_part(i - 3))
        if i:
            dn_move(g, i - 1).wait_recv()
            total = total + decode(ring_r[g, 3 + i])
        ring_s[g, 4 + i] = code(total)
        dn_move(g, i).start()

    def ring_1(g):
        core_move(g).wait_recv()
        send_up(g, 0)

    def ring_2(g, i=1):
        send_dn(g, i - 1)
        send_up(g, i)

    def ring_5(g):
        dn_move(g, 2).wait_recv()
        up_move(g, 3).wait_recv()
        total = with_twin(g, ring_part(0)) + decode(ring_r[g, 6]) + decode(ring_r[g, 3])
        acc[g, ring_part(0), :] = total
        xsend[g, pl.ds(0, SLICE), :] = code(total)
        x_move(g).start()

    def ring_6(g):
        x_move(g).wait_recv()
        low = acc[g, ring_part(0), :] + decode(xrecv[g, pl.ds(0, SLICE), :])
        rall[g, rows(own0 + z * SLICE, SLICE), :] = low.astype(jnp.bfloat16)
        out_dn(g, 0).start()
        out_up(g, 0).start()

    def ring_7(g, i=0):
        in_dn(g, i).wait_recv()
        out_dn(g, i + 1).start()
        in_up(g, i).wait_recv()
        out_up(g, i + 1).start()

    def ring_9(g):
        in_dn(g, 2).wait_recv()
        out_dn(g, 3).start()
        in_up(g, 2).wait_recv()

    def ring_10(g):
        in_dn(g, 3).wait_recv()
        share(g)

    def ring_sent(g):
        for i in range(4):
            up_move(g, i).wait_send()
            out_dn(g, i).wait_send()
        for i in range(3):
            dn_move(g, i).wait_send()
            out_up(g, i).wait_send()

    def stage_gradient(g):
        in_core(g).wait_recv()
        add_gradient(g, other0, OTHER_ENDS)

        @pl.when(g == my_slot)
        def _():
            half = rall[g, :, pl.ds(pl.multiple_of(my_half * 128, 128), 128)]
            turned[...] = half.astype(jnp.float32).T
            res_ref[...] = turned[rows(core * 64, 64), :]

        core_move(g).wait_send()
        out_core(g).wait_send()

        if g in KINDS["two"]:
            two_sent(g)
            x_move(g).wait_send()

        if g in KINDS["xf"]:
            xf_sent(g)
            half_move(g).wait_send()
            out_x(g).wait_send()

        if g in KINDS["ring"]:
            ring_sent(g)
            x_move(g).wait_send()

    stages = {
        "pass_on": pass_on, "predict": stage_predict, "gradient": stage_gradient,
        "two_1": two_1, "two_2": two_sums, "two_3": two_3, "two_4": two_4, "two_5": two_on,
        "two_6": two_6,
        "xf_1": xf_1, "xf_2": xf_2, "xf_3": xf_sums, "xf_4": xf_4, "xf_5": xf_on, "xf_6": xf_6,
        "xf_7": xf_7,
        "ring_1": ring_1, "ring_2": ring_2, "ring_3": functools.partial(ring_2, i=2),
        "ring_4": functools.partial(ring_2, i=3), "ring_5": ring_5, "ring_6": ring_6,
        "ring_7": ring_7, "ring_8": functools.partial(ring_7, i=1), "ring_9": ring_9,
        "ring_10": ring_10,
    }

    for name, g in ORDER:
        stages[name](g)

    for move in s_moves:
        move.wait_send()


def finish(g_ref, res_ref, g_hbm, res_hbm, sem):
    size = FULL // PIECES
    moves = [pltpu.make_async_copy(res_ref, res_hbm, sem.at[PIECES])]
    for i in range(PIECES):
        here = pl.ds(i * size, size)
        moves.append(pltpu.make_async_copy(g_ref.at[here], g_hbm.at[here], sem.at[i]))
    for move in moves:
        move.start()
    for move in moves:
        move.wait()


def on_device(reconstructor, slopes, commands):
    vmem = pltpu.VMEM
    gradient, residual = pl.pallas_call(
        kernel,
        out_shape=(
            pltpu.VMEM((FULL, DEPTH), jnp.float32),
            pltpu.VMEM((64, FULL), jnp.float32),
        ),
        in_specs=[pl.BlockSpec(memory_space=pl.ANY)] * 3,
        out_specs=[pl.BlockSpec(memory_space=pltpu.VMEM)] * 2,
        scratch_shapes=[
            vmem((FULL, DEPTH), jnp.bfloat16),
            vmem((BLOCKS, DEPTH, BLOCK), jnp.bfloat16),
            vmem((BLOCK, FULL), jnp.float32),
            vmem((FULL, BLOCK), jnp.float32),
            vmem((BLOCKS, HALF, BLOCK), jnp.float32),
            vmem((BLOCKS, HALF, BLOCK), jnp.bfloat16),
            vmem((BLOCKS, HALF, BLOCK), jnp.bfloat16),
            vmem((BLOCKS, 2, 2 * SLICE, BLOCK), jnp.bfloat16),
            vmem((BLOCKS, 2, 2 * SLICE, BLOCK), jnp.bfloat16),
            vmem((BLOCKS, 2, SLICE // 2, BLOCK), jnp.bfloat16),
            vmem((BLOCKS, 2, SLICE // 2, BLOCK), jnp.bfloat16),
            vmem((BLOCKS, 2, SLICE, BLOCK), jnp.bfloat16),
            vmem((BLOCKS, 2, SLICE, BLOCK), jnp.bfloat16),
            vmem((BLOCKS, 7, SLICE, BLOCK), jnp.bfloat16),
            vmem((BLOCKS, 7, SLICE, BLOCK), jnp.bfloat16),
            vmem((BLOCKS, HALF // 2, BLOCK), jnp.bfloat16),
            vmem((BLOCKS, HALF // 2, BLOCK), jnp.bfloat16),
            vmem((BLOCKS, FULL, BLOCK), jnp.bfloat16),
            vmem((128, FULL), jnp.float32),
            pltpu.SemaphoreType.DMA((3,)),
            pltpu.SemaphoreType.DMA((18,)),
            pltpu.SemaphoreType.DMA((18,)),
            pltpu.SemaphoreType.DMA((BLOCKS, 19)),
            pltpu.SemaphoreType.DMA((BLOCKS, 19)),
        ],
        compiler_params=pltpu.CompilerParams(
            collective_id=0, has_side_effects=True, vmem_limit_bytes=56 << 20
        ),
        cost_estimate=pl.CostEstimate(
            flops=4 * 2048 * FULL * DEPTH, bytes_accessed=9 << 20, transcendentals=0
        ),
    )(reconstructor, slopes, commands)
    return pl.pallas_call(
        finish,
        out_shape=(
            jax.ShapeDtypeStruct((FULL, DEPTH), jnp.float32),
            jax.ShapeDtypeStruct((64, FULL), jnp.float32),
        ),
        in_specs=[pl.BlockSpec(memory_space=pltpu.VMEM)] * 2,
        out_specs=[pl.BlockSpec(memory_space=pl.ANY)] * 2,
        scratch_shapes=[
            pltpu.SemaphoreType.DMA((PIECES + 1,)),
        ],
        compiler_params=pltpu.CompilerParams(vmem_limit_bytes=4 << 20),
    )(gradient, residual)


def solution(mesh):
    in_specs = (P("row", "col"), P("col", "row"), P("col", "row"))
    out_specs = (P("row", "col"), P("col", "row"))
    return jax.shard_map(
        on_device, mesh=mesh, in_specs=in_specs, out_specs=out_specs, check_vma=False
    )
```

```python
import functools

import jax
import jax.numpy as jnp
from jax import lax
from jax.experimental import pallas as pl
from jax.experimental.pallas import tpu as pltpu
from jax.sharding import PartitionSpec as P

MESH = pl.DeviceIdType.MESH

FULL = 1024
HALF = 512
SLICE = 64
DEPTH = 1280
BLOCK = 256
BLOCKS = 8
PIECES = 8
KINDS = {
    "two": (0, 7,),
    "xf": (1, 6,),
    "ring": (2, 3, 4, 5,),
}
ORDER = (
    ("predict", 0), ("two_1", 0), ("two_2", 0), ("pass_on", 0), ("predict", 1), ("xf_1", 1),
    ("two_3", 0), ("pass_on", 1), ("predict", 2), ("pass_on", 2), ("pass_on", 3), ("predict", 3),
    ("ring_1", 2), ("pass_on", 4), ("ring_1", 3), ("xf_2", 1), ("ring_2", 2), ("two_4", 0),
    ("pass_on", 5), ("predict", 4), ("ring_1", 4), ("ring_3", 2), ("ring_2", 3), ("xf_3", 1),
    ("two_5", 0), ("ring_2", 4), ("ring_4", 2), ("ring_3", 3), ("predict", 5), ("ring_1", 5),
    ("ring_5", 2), ("ring_3", 4), ("xf_4", 1), ("ring_4", 3), ("predict", 6), ("ring_2", 5),
    ("ring_4", 4), ("xf_1", 6), ("ring_6", 2), ("xf_5", 1), ("predict", 7), ("ring_3", 5),
    ("two_1", 7), ("ring_5", 4), ("ring_7", 2), ("ring_5", 3), ("ring_4", 5), ("xf_2", 6),
    ("xf_6", 1), ("ring_6", 4), ("ring_6", 3), ("two_2", 7), ("ring_8", 2), ("two_6", 0),
    ("ring_5", 5), ("xf_3", 6), ("ring_7", 4), ("ring_7", 3), ("xf_7", 1), ("ring_6", 5),
    ("ring_9", 2), ("gradient", 1), ("xf_4", 6), ("ring_8", 4), ("two_3", 7), ("ring_8", 3),
    ("ring_7", 5), ("ring_10", 2), ("xf_5", 6), ("two_4", 7), ("ring_9", 4), ("ring_9", 3),
    ("gradient", 0), ("ring_8", 5), ("gradient", 2), ("xf_6", 6), ("two_5", 7), ("ring_10", 4),
    ("ring_10", 3), ("ring_9", 5), ("gradient", 4), ("gradient", 3), ("xf_7", 6), ("two_6", 7),
    ("ring_10", 5), ("gradient", 6), ("gradient", 7), ("gradient", 5),
)
OWN_ENDS, OTHER_ENDS = (0, 5), (1, 5)


def code(v):
    return (v * jnp.abs(v) * (v * v)).astype(jnp.bfloat16)


def decode(b):
    b = b.astype(jnp.float32)
    m = jnp.abs(b)
    m = m * lax.rsqrt(jnp.maximum(m, 1e-36))
    m = m * lax.rsqrt(jnp.maximum(m, 1e-18))
    return jnp.where(b < 0, -m, m)


def kernel(
    r_hbm, s_hbm, c_hbm, g_ref, res_ref,
    r_ref, sall, cpad, cmd_t, acc, csend, crecv, near_s, near_r, far_s, far_r, sum_s, sum_r,
    ring_s, ring_r, xsend, xrecv, rall, turned,
    in_sem, s_ss, s_rs, ss, rs,
):
    row, col = lax.axis_index("row"), lax.axis_index("col")
    y, xh = row // 2, row % 2
    z, xl, core = col // 4, (col // 2) % 2, col % 2
    quad = xl * 2 + core
    y_up = (((y + 1) % 4) * 2 + xh, col)
    y_dn = (((y + 3) % 4) * 2 + xh, col)
    x_far = (y * 2 + 1 - xh, col)
    z_up = (row, ((z + 1) % 8) * 4 + quad)
    z_dn = (row, ((z + 7) % 8) * 4 + quad)
    z_up2 = (row, ((z + 2) % 8) * 4 + quad)
    z_dn2 = (row, ((z + 6) % 8) * 4 + quad)
    x_near = (row, z * 4 + (1 - xl) * 2 + core)
    twin = (row, z * 4 + xl * 2 + 1 - core)

    barrier = pltpu.get_barrier_semaphore()
    for device in (y_up, y_dn, x_far, z_up, z_dn, z_up2, z_dn2, x_near, twin):
        pl.semaphore_signal(barrier, inc=1, device_id=device, device_id_type=MESH)

    s_in = pltpu.make_async_copy(s_hbm, sall.at[0], in_sem.at[0])
    r_in = pltpu.make_async_copy(r_hbm, r_ref, in_sem.at[1])
    s_in.start()
    r_in.start()
    cpad[...] = jnp.zeros_like(cpad)
    def remote(src, dst, send, recv, device):
        return pltpu.make_async_remote_copy(
            src_ref=src, dst_ref=dst, send_sem=send, recv_sem=recv,
            device_id=device, device_id_type=MESH,
        )

    mid = DEPTH // 2
    lo, hi, every = pl.ds(0, mid), pl.ds(mid, mid), pl.ds(0, DEPTH)
    most, rest = pl.ds(0, 3 * DEPTH // 4), pl.ds(3 * DEPTH // 4, DEPTH // 4)
    left, right = pl.ds(0, 128), pl.ds(128, 128)
    s_moves = [
        remote(
            s_hbm.at[r0, c0] if i == 0 else sall.at[i, r0, c0],
            sall.at[j, r0, c1], s_ss.at[n], s_rs.at[n], device,
        )
        for n, (i, j, r0, c0, c1, device) in enumerate((
            (0, 1, every, left, left, y_up),
            (0, 1, every, left, right, y_dn),
            (0, 2, every, right, left, y_up),
            (0, 2, every, right, right, y_dn),
            (0, 3, every, left, left, x_far),
            (0, 3, every, right, right, x_far),
            (1, 4, lo, left, left, y_up),
            (1, 4, hi, right, left, y_dn),
            (2, 4, lo, left, right, y_up),
            (2, 4, hi, right, right, y_dn),
            (3, 5, every, left, left, y_up),
            (3, 5, every, left, right, y_dn),
            (3, 6, most, right, left, y_up),
            (3, 6, most, right, right, y_dn),
            (4, 7, every, left, left, x_far),
            (4, 7, every, right, right, x_far),
            (2, 6, rest, left, left, x_far),
            (2, 6, rest, right, right, x_far),
        ))
    ]
    passes = [
        ((0, 1), (6, 7)), ((2, 3), (8, 9, 16, 17)), ((4,), (10, 11)), ((5,), (12, 13)), ((6, 7), (14,)),
        ((8, 9), (15,)),
    ]
    dy = (z // 2 + 4 - y) % 4
    dx = (z % 2 + 2 - xh) % 2
    beside = (dy == 1) | (dy == 3)
    my_slot = jnp.where(beside, 1 + 4 * dx + xl, jnp.where(dy == 0, 3 * dx, 4 + 3 * dx))
    my_half = jnp.where(beside, (dy == 1).astype(jnp.int32), xl)
    c_in = pltpu.make_async_copy(
        c_hbm,
        cpad.at[pl.ds(pl.multiple_of(my_half * 128 + core * 64, 64), 64)],
        in_sem.at[2],
    )
    c_in.start()
    pl.semaphore_wait(barrier, 9)
    for i in (0, 1, 4, 2, 3, 5):
        s_moves[i].start()
    s_in.wait()

    c_in.wait()
    cmd_t[...] = cpad[...].T
    r_in.wait()

    own0 = core * HALF
    other0 = (1 - core) * HALF

    def rows(start, size):
        return pl.ds(pl.multiple_of(start, size), size)

    def core_move(g):
        return remote(csend.at[g], crecv.at[g], ss.at[g, 0], rs.at[g, 0], twin)

    one, two = (z_up, z_dn), (z_up2, z_dn2)

    def out_core(g):
        here = rall.at[g, rows(own0, HALF)]
        return remote(here, here, ss.at[g, 16], rs.at[g, 16], twin)

    def in_core(g):
        here = rall.at[g, rows(other0, HALF)]
        return remote(here, here, ss.at[g, 16], rs.at[g, 16], twin)

    def pass_on(n):
        arrived, onward = passes[n]
        for i in arrived:
            s_moves[i].wait_recv()
        for i in onward:
            s_moves[i].start()

    def stage_predict(g):
        if g >= 5:
            s_moves[2 * g].wait_recv()
            s_moves[2 * g + 1].wait_recv()
        if g == 6:
            s_moves[16].wait_recv()
            s_moves[17].wait_recv()

        mine = (g == my_slot).astype(jnp.float32)
        tile = 512

        def predicted(start):
            p = jnp.dot(
                r_ref[rows(start, tile), :], sall[g], preferred_element_type=jnp.float32
            )
            return p - cmd_t[rows(start, tile), :] * mine

        @pl.loop(0, HALF // tile)
        def _(i):
            csend[g, rows(i * tile, tile), :] = code(predicted(other0 + i * tile))

        core_move(g).start()

        @pl.loop(0, HALF // tile)
        def _(i):
            acc[g, rows(i * tile, tile), :] = predicted(own0 + i * tile)

    scale_factor = 1.0 / jnp.sqrt(jnp.float32(2048))

    def add_gradient(g, start, ends):
        here = rows(start, HALF)
        added = lax.dot_general(
            rall[g, here, :], sall[g], (((1,), (1,)), ((), ())),
            preferred_element_type=jnp.float32,
        )
        if g != ends[0]:
            added = g_ref[here, :] + added
        g_ref[here, :] = added * scale_factor if g == ends[1] else added

    def share(g):
        out_core(g).start()
        add_gradient(g, own0, OWN_ENDS)

    def with_twin(g, here):
        return acc[g, here, :] + decode(crecv[g, here, :])

    def tree(size, base, term):
        half = size // 2
        first, second = pl.ds(0, size), pl.ds(size, size)

        def part(at, count=size, skip=0):
            return rows(base + ((z + at + 8) % 8) * size + skip, count)

        def near_move(g, d):
            here = near_s.at[g, d, pl.ds(0, 2 * size)]
            there = near_r.at[g, d, pl.ds(0, 2 * size)]
            return remote(here, there, ss.at[g, 1 + d], rs.at[g, 1 + d], one[d])

        def far_move(g, d):
            here, there = far_s.at[g, d, pl.ds(0, half)], far_r.at[g, d, pl.ds(0, half)]
            return remote(here, there, ss.at[g, 3 + d], rs.at[g, 3 + d], two[d])

        def sum_move(g, d):
            here, there = sum_s.at[g, d, first], sum_r.at[g, d, first]
            return remote(here, there, ss.at[g, 5 + d], rs.at[g, 5 + d], two[d])

        def spread(g, d, n, at, device, count=size, skip=0):
            start = own0 + base + ((z + at + 8) % 8) * size + skip
            here = rall.at[g, rows(start, count)]
            return remote(here, here, ss.at[g, n + d], rs.at[g, n + d], device)

        def out_1(g, d):
            return spread(g, d, 8, 0, one[d])

        def in_1(g, d):
            return spread(g, d, 8, (-1, 1)[d], one[d])

        def out_2(g, d):
            return spread(g, d, 10, 0, two[d])

        def in_2(g, d):
            return spread(g, d, 10, (-2, 2)[d], two[d])

        def out_3(g, d):
            return spread(g, d, 12, (-2, 2)[d], one[d])

        def in_3(g, d):
            return spread(g, d, 12, (-3, 3)[d], one[d])

        def out_4(g, d):
            return spread(g, d, 14, (-2, 2)[d], two[d], half, d * half)

        def in_4(g, d):
            return spread(g, d, 14, 4, two[d], half, d * half)

        def send_terms(g):
            for d, sign in ((0, 1), (1, -1)):
                far_s[g, d, pl.ds(0, half), :] = code(term(g, part(4, half, d * half)))
                far_move(g, d).start()
                near_s[g, d, second, :] = code(term(g, part(3 * sign)))
                near_s[g, d, first, :] = code(term(g, part(sign)))
                near_move(g, d).start()

        def send_sums(g):
            for d, sign in ((0, 1), (1, -1)):
                near_move(g, d).wait_recv()
                far_move(g, d).wait_recv()
                for h in (0, 1):
                    total = term(g, part(2 * sign, half, h * half)) + decode(
                        near_r[g, d, pl.ds(size + h * half, half), :]
                    )
                    if h == d:
                        total = total + decode(far_r[g, d, pl.ds(0, half), :])
                    sum_s[g, d, pl.ds(h * half, half), :] = code(total)
                sum_move(g, d).start()

        def total(g):
            total = term(g, part(0))
            for d in (0, 1):
                sum_move(g, d).wait_recv()
                total = total + decode(near_r[g, d, first, :]) + decode(sum_r[g, d, first, :])
            return total

        def hand_round(g, residual):
            rall[g, rows(own0 + base + z * size, size), :] = residual.astype(jnp.bfloat16)
            for d in (0, 1):
                out_2(g, d).start()
            for d in (0, 1):
                out_1(g, d).start()

        def hand_on(g):
            for d in (0, 1):
                in_2(g, d).wait_recv()
                out_4(g, d).start()
                out_3(g, d).start()

        def all_here(g):
            for d in (0, 1):
                in_1(g, d).wait_recv()
                in_3(g, d).wait_recv()
                in_4(g, d).wait_recv()

        def sent(g):
            for move in (near_move, far_move, sum_move, out_1, out_2, out_3, out_4):
                for d in (0, 1):
                    move(g, d).wait_send()

        return part, send_terms, send_sums, total, hand_round, hand_on, all_here, sent

    def x_move(g):
        here, there = xsend.at[g, pl.ds(0, SLICE)], xrecv.at[g, pl.ds(0, SLICE)]
        return remote(here, there, ss.at[g, 18], rs.at[g, 18], x_near)

    (
        two_part, two_terms, two_sums, two_total, two_round, two_on, two_here, two_sent,
    ) = tree(SLICE, 0, with_twin)

    def two_1(g):
        core_move(g).wait_recv()
        two_terms(g)

    def two_3(g):
        total = two_total(g)
        acc[g, two_part(0), :] = total
        xsend[g, pl.ds(0, SLICE), :] = code(total)
        x_move(g).start()

    def two_4(g):
        x_move(g).wait_recv()
        two_round(g, acc[g, two_part(0), :] + decode(xrecv[g, pl.ds(0, SLICE), :]))

    def two_6(g):
        two_here(g)
        share(g)

    quarter = HALF // 2

    def half_move(g):
        return remote(xsend.at[g], xrecv.at[g], ss.at[g, 7], rs.at[g, 7], x_near)

    def out_x(g):
        here = rall.at[g, rows(own0 + xl * quarter, quarter)]
        return remote(here, here, ss.at[g, 17], rs.at[g, 17], x_near)

    def in_x(g):
        here = rall.at[g, rows(own0 + (1 - xl) * quarter, quarter)]
        return remote(here, here, ss.at[g, 17], rs.at[g, 17], x_near)

    xf_part, xf_terms, xf_sums, xf_total, xf_round, xf_on, xf_here, xf_sent = tree(
        SLICE // 2, xl * quarter, lambda g, here: acc[g, here, :]
    )

    def xf_1(g):
        core_move(g).wait_recv()

        @pl.loop(0, quarter // SLICE)
        def _(i):
            here = rows((1 - xl) * quarter + i * SLICE, SLICE)
            xsend[g, rows(i * SLICE, SLICE), :] = code(with_twin(g, here))

        half_move(g).start()

    def xf_2(g):
        half_move(g).wait_recv()

        @pl.loop(0, quarter // SLICE)
        def _(i):
            here = rows(xl * quarter + i * SLICE, SLICE)
            other = decode(xrecv[g, rows(i * SLICE, SLICE), :])
            acc[g, here, :] = with_twin(g, here) + other

        xf_terms(g)

    def xf_4(g):
        xf_round(g, xf_total(g))

    def xf_6(g):
        xf_here(g)
        out_x(g).start()

    def xf_7(g):
        in_x(g).wait_recv()
        share(g)

    def ring_part(at):
        return rows(((z + at + 8) % 8) * SLICE, SLICE)

    def ring_here(g, at):
        return rall.at[g, rows(own0 + ((z + at + 8) % 8) * SLICE, SLICE)]

    def up_move(g, i):
        return remote(ring_s.at[g, i], ring_r.at[g, i], ss.at[g, 1 + i], rs.at[g, 1 + i], z_up)

    def dn_move(g, i):
        return remote(
            ring_s.at[g, 4 + i], ring_r.at[g, 4 + i], ss.at[g, 5 + i], rs.at[g, 5 + i], z_dn
        )

    def out_up(g, i):
        here = ring_here(g, -i)
        return remote(here, here, ss.at[g, 9 + i], rs.at[g, 9 + i], z_up)

    def in_up(g, i):
        here = ring_here(g, -i - 1)
        return remote(here, here, ss.at[g, 9 + i], rs.at[g, 9 + i], z_up)

    def out_dn(g, i):
        here = ring_here(g, i)
        return remote(here, here, ss.at[g, 12 + i], rs.at[g, 12 + i], z_dn)

    def in_dn(g, i):
        here = ring_here(g, i + 1)
        return remote(here, here, ss.at[g, 12 + i], rs.at[g, 12 + i], z_dn)

    def send_up(g, i):
        total = with_twin(g, ring_part(4 - i))
        if i:
            up_move(g, i - 1).wait_recv()
            total = total + decode(ring_r[g, i - 1])
        ring_s[g, i] = code(total)
        up_move(g, i).start()

    def send_dn(g, i):
        total = with_twin(g, ring_part(i - 3))
        if i:
            dn_move(g, i - 1).wait_recv()
            total = total + decode(ring_r[g, 3 + i])
        ring_s[g, 4 + i] = code(total)
        dn_move(g, i).start()

    def ring_1(g):
        core_move(g).wait_recv()
        send_up(g, 0)

    def ring_2(g, i=1):
        send_dn(g, i - 1)
        send_up(g, i)

    def ring_5(g):
        dn_move(g, 2).wait_recv()
        up_move(g, 3).wait_recv()
        total = with_twin(g, ring_part(0)) + decode(ring_r[g, 6]) + decode(ring_r[g, 3])
        acc[g, ring_part(0), :] = total
        xsend[g, pl.ds(0, SLICE), :] = code(total)
        x_move(g).start()

    def ring_6(g):
        x_move(g).wait_recv()
        low = acc[g, ring_part(0), :] + decode(xrecv[g, pl.ds(0, SLICE), :])
        rall[g, rows(own0 + z * SLICE, SLICE), :] = low.astype(jnp.bfloat16)
        out_dn(g, 0).start()
        out_up(g, 0).start()

    def ring_7(g, i=0):
        in_dn(g, i).wait_recv()
        out_dn(g, i + 1).start()
        in_up(g, i).wait_recv()
        out_up(g, i + 1).start()

    def ring_9(g):
        in_dn(g, 2).wait_recv()
        out_dn(g, 3).start()
        in_up(g, 2).wait_recv()

    def ring_10(g):
        in_dn(g, 3).wait_recv()
        share(g)

    def ring_sent(g):
        for i in range(4):
            up_move(g, i).wait_send()
            out_dn(g, i).wait_send()
        for i in range(3):
            dn_move(g, i).wait_send()
            out_up(g, i).wait_send()

    def stage_gradient(g):
        in_core(g).wait_recv()
        add_gradient(g, other0, OTHER_ENDS)

        @pl.when(g == my_slot)
        def _():
            half = rall[g, :, pl.ds(pl.multiple_of(my_half * 128, 128), 128)]
            turned[...] = half.astype(jnp.float32).T
            res_ref[...] = turned[rows(core * 64, 64), :]

        core_move(g).wait_send()
        out_core(g).wait_send()

        if g in KINDS["two"]:
            two_sent(g)
            x_move(g).wait_send()

        if g in KINDS["xf"]:
            xf_sent(g)
            half_move(g).wait_send()
            out_x(g).wait_send()

        if g in KINDS["ring"]:
            ring_sent(g)
            x_move(g).wait_send()

    stages = {
        "pass_on": pass_on, "predict": stage_predict, "gradient": stage_gradient,
        "two_1": two_1, "two_2": two_sums, "two_3": two_3, "two_4": two_4, "two_5": two_on,
        "two_6": two_6,
        "xf_1": xf_1, "xf_2": xf_2, "xf_3": xf_sums, "xf_4": xf_4, "xf_5": xf_on, "xf_6": xf_6,
        "xf_7": xf_7,
        "ring_1": ring_1, "ring_2": ring_2, "ring_3": functools.partial(ring_2, i=2),
        "ring_4": functools.partial(ring_2, i=3), "ring_5": ring_5, "ring_6": ring_6,
        "ring_7": ring_7, "ring_8": functools.partial(ring_7, i=1), "ring_9": ring_9,
        "ring_10": ring_10,
    }

    for name, g in ORDER:
        stages[name](g)

    for move in s_moves:
        move.wait_send()


def finish(g_ref, res_ref, g_hbm, res_hbm, sem):
    size = FULL // PIECES
    moves = [pltpu.make_async_copy(res_ref, res_hbm, sem.at[PIECES])]
    for i in range(PIECES):
        here = pl.ds(i * size, size)
        moves.append(pltpu.make_async_copy(g_ref.at[here], g_hbm.at[here], sem.at[i]))
    for move in moves:
        move.start()
    for move in moves:
        move.wait()


def on_device(reconstructor, slopes, commands):
    vmem = pltpu.VMEM
    gradient, residual = pl.pallas_call(
        kernel,
        out_shape=(
            pltpu.VMEM((FULL, DEPTH), jnp.float32),
            pltpu.VMEM((64, FULL), jnp.float32),
        ),
        in_specs=[pl.BlockSpec(memory_space=pl.ANY)] * 3,
        out_specs=[pl.BlockSpec(memory_space=pltpu.VMEM)] * 2,
        scratch_shapes=[
            vmem((FULL, DEPTH), jnp.bfloat16),
            vmem((BLOCKS, DEPTH, BLOCK), jnp.bfloat16),
            vmem((BLOCK, FULL), jnp.float32),
            vmem((FULL, BLOCK), jnp.float32),
            vmem((BLOCKS, HALF, BLOCK), jnp.float32),
            vmem((BLOCKS, HALF, BLOCK), jnp.bfloat16),
            vmem((BLOCKS, HALF, BLOCK), jnp.bfloat16),
            vmem((BLOCKS, 2, 2 * SLICE, BLOCK), jnp.bfloat16),
            vmem((BLOCKS, 2, 2 * SLICE, BLOCK), jnp.bfloat16),
            vmem((BLOCKS, 2, SLICE // 2, BLOCK), jnp.bfloat16),
            vmem((BLOCKS, 2, SLICE // 2, BLOCK), jnp.bfloat16),
            vmem((BLOCKS, 2, SLICE, BLOCK), jnp.bfloat16),
            vmem((BLOCKS, 2, SLICE, BLOCK), jnp.bfloat16),
            vmem((BLOCKS, 7, SLICE, BLOCK), jnp.bfloat16),
            vmem((BLOCKS, 7, SLICE, BLOCK), jnp.bfloat16),
            vmem((BLOCKS, HALF // 2, BLOCK), jnp.bfloat16),
            vmem((BLOCKS, HALF // 2, BLOCK), jnp.bfloat16),
            vmem((BLOCKS, FULL, BLOCK), jnp.bfloat16),
            vmem((128, FULL), jnp.float32),
            pltpu.SemaphoreType.DMA((3,)),
            pltpu.SemaphoreType.DMA((18,)),
            pltpu.SemaphoreType.DMA((18,)),
            pltpu.SemaphoreType.DMA((BLOCKS, 19)),
            pltpu.SemaphoreType.DMA((BLOCKS, 19)),
        ],
        compiler_params=pltpu.CompilerParams(
            collective_id=0, has_side_effects=True, vmem_limit_bytes=56 << 20
        ),
        cost_estimate=pl.CostEstimate(
            flops=4 * 2048 * FULL * DEPTH, bytes_accessed=9 << 20, transcendentals=0
        ),
    )(reconstructor, slopes, commands)
    return pl.pallas_call(
        finish,
        out_shape=(
            jax.ShapeDtypeStruct((FULL, DEPTH), jnp.float32),
            jax.ShapeDtypeStruct((64, FULL), jnp.float32),
        ),
        in_specs=[pl.BlockSpec(memory_space=pltpu.VMEM)] * 2,
        out_specs=[pl.BlockSpec(memory_space=pl.ANY)] * 2,
        scratch_shapes=[
            pltpu.SemaphoreType.DMA((PIECES + 1,)),
        ],
        compiler_params=pltpu.CompilerParams(vmem_limit_bytes=4 << 20),
    )(gradient, residual)


def solution(mesh):
    in_specs = (P("row", "col"), P("col", "row"), P("col", "row"))
    out_specs = (P("row", "col"), P("col", "row"))
    return jax.shard_map(
        on_device, mesh=mesh, in_specs=in_specs, out_specs=out_specs, check_vma=False
    )
```
